32 devices in a mesh: dp: 16 (over z, y, core), mp: 2 (over x).
Axes of the slice: x: 2, y: 2, z: 4, core: 2. Of those that a mesh axis runs over, the one named last changes fastest.
Arguments:
- tokens: bfloat16 [256, 6144], P('dp', 'mp'), may hold values from -6 to 6
- norm_gain: float32 [6144], P('mp'), may hold values from 0.25 to 1.75
- w_up: bfloat16 [6144, 24576], P('mp', 'dp'), may hold values from -0.078125 to 0.078125
- cotangent: bfloat16 [256, 24576], P('mp', 'dp'), may hold values from -32 to 32
Outputs:
- sharp_grad: float32 [6144, 24576], P('mp', 'dp')
The draws below stay inside these ranges and needn't reach their ends.
All inputs are finite; a program needn't handle non-finite values.
Results may differ from the reference program's by a relative error of at most 0.0048.
Values may be sent and summed in bfloat16 or wider, within the bound.
A program may use at most 64 MiB of HBM per device.

```python
import math
import jax
import jax.numpy as jnp
from jax import lax

D = 6144
FF = 24576
TOKENS = 256


def token_signs(key):
    key = jax.random.fold_in(key, 101)
    flips = jax.random.randint(key, (TOKENS, 1), 0, 2)
    return (2 * flips - 1).astype(jnp.float32)


def signed_profile(key, length, lower, upper):
    keys = jax.random.split(key, 2)
    magnitude = jax.random.uniform(keys[0], (1, length), jnp.float32, lower, upper)
    flips = jax.random.randint(keys[1], (1, length), 0, 2)
    return magnitude * (2 * flips - 1).astype(jnp.float32)


def window_mask(key, length, width):
    start = jax.random.randint(key, (), 0, length - width + 1)
    position = jnp.arange(length, dtype=jnp.int32)
    inside = (position >= start) & (position < start + width)
    return inside.astype(jnp.float32)[None, :]


def draw_tokens(key, part):
    signs = token_signs(key)
    key = jax.random.fold_in(key, 5)
    keys = jax.random.split(key, 3)
    profile = signed_profile(keys[0], D, 0.4, 1.0) * window_mask(keys[1], D, D // 8)
    base = jnp.clip(jax.random.normal(keys[2], (TOKENS, D), jnp.float32), -4.0, 4.0)
    return (base + signs * profile).astype(jnp.bfloat16)


def draw_cotangent(key, part):
    signs = token_signs(key)
    key = jax.random.fold_in(key, 7)
    keys = jax.random.split(key, 6)
    row_scale = jnp.exp(jax.random.uniform(keys[0], (TOKENS, 1), jnp.float32, math.log(0.3), math.log(3.0)))
    position = jnp.arange(FF, dtype=jnp.float32) / FF
    col_scale = jnp.exp(math.log(3.0) * position[None, :] + jax.random.uniform(keys[1], (1, FF), jnp.float32, -0.5, 0.5))
    coherent = signed_profile(keys[4], FF, 0.5, 1.2) * window_mask(keys[5], FF, FF // 16)
    base = jnp.clip(jax.random.normal(keys[2], (TOKENS, FF), jnp.float32), -4.0, 4.0)
    return (0.5 * base * row_scale * col_scale + signs * coherent).astype(jnp.bfloat16)


def level_of(rng, extent, shards, smallest, top_value):
    level = 1.0
    for dim, blocks in shards:
        heights = jax.random.uniform(jax.random.fold_in(jax.random.fold_in(rng, 6), dim), (blocks,), jnp.float32, smallest / len(shards), top_value / len(shards))
        level = level * jnp.repeat(jnp.exp(heights), extent[dim] // blocks).reshape((-1,) + (1,) * (len(extent) - 1 - dim))
    return level


def centred(rng, shape, deviation, bound, cuts=(), kind=jnp.bfloat16):
    entries = jax.random.normal(rng, shape, jnp.float32) * deviation
    if len(cuts) > 0:
        entries = level_of(rng, shape, cuts, -0.22, 0.18) * entries
    return jnp.clip(entries, min=-bound, max=bound).astype(kind)


def setup_inputs(seed: int = 0) -> dict:
    arg_keys = jax.random.split(jax.random.key(seed), 5)
    tokens = draw_tokens(jax.random.fold_in(arg_keys[4], 71), 0)
    norm_gain = jnp.clip(1.0 + 0.15 * jax.random.normal(arg_keys[1], (D,), jnp.float32), 0.25, 1.75)
    w_up = centred(arg_keys[2], (D, FF), D ** -0.5, 0.078125, ((0, 2), (1, 16)))
    cotangent = draw_cotangent(jax.random.fold_in(arg_keys[4], 71), 0)
    return {"tokens": tokens, "norm_gain": norm_gain, "w_up": w_up, "cotangent": cotangent}


def gelu_slope(value):
    cdf = 0.5 * (1.0 + lax.erf(value * (1.0 / math.sqrt(2.0))))
    dens = jnp.exp(-0.5 * value * value) * (1.0 / math.sqrt(2.0 * math.pi))
    return cdf + value * dens

def weight_grad(normed, weights, cotangent):
    pre = jnp.dot(normed, weights, preferred_element_type=jnp.float32)
    scale = 1.0 / math.sqrt(TOKENS)
    slope = (cotangent.astype(jnp.float32) * gelu_slope(pre) * scale).astype(jnp.bfloat16)
    return jnp.dot(normed.T, slope, preferred_element_type=jnp.float32)

def reference(tokens, norm_gain, w_up, cotangent):
    values = tokens.astype(jnp.float32)
    mean = lax.optimization_barrier(jnp.sum(values, axis=1)) / D
    var = lax.optimization_barrier(jnp.sum(values * values, axis=1)) / D - mean * mean
    normed = ((values - mean[:, None]) * lax.rsqrt(var[:, None] + 1e-06) * norm_gain[None, :]).astype(jnp.bfloat16)
    ascent = weight_grad(normed, w_up, cotangent)
    size = jnp.sqrt(jnp.sum(ascent * ascent)) + 1e-12
    radius = 0.5 * math.sqrt(FF)
    perturbed = (w_up.astype(jnp.float32) + radius * ascent / size).astype(jnp.bfloat16)
    return weight_grad(normed, perturbed, cotangent)
```

```python
import functools
import math

import jax
import jax.numpy as jnp
from jax import lax
from jax.experimental import pallas as pl
from jax.experimental.pallas import tpu as pltpu
from jax.sharding import PartitionSpec as P

FF = 24576
MESH = pl.DeviceIdType.MESH
F32 = jnp.float32
BF16 = jnp.bfloat16


def gelu_slope(value):
    cdf = 0.5 * (1.0 + lax.erf(value * (1.0 / math.sqrt(2.0))))
    dens = jnp.exp(-0.5 * value * value) * (1.0 / math.sqrt(2.0 * math.pi))
    return cdf + value * dens


def remote(src, dst, send_sem, recv_sem, device):
    return pltpu.make_async_remote_copy(
        src_ref=src, dst_ref=dst, send_sem=send_sem, recv_sem=recv_sem,
        device_id=device, device_id_type=MESH,
    )


def slopes_kernel(
    cfg,
    tok_ref, gain_ref, w_hbm, cot_hbm,
    nt_ref, pre_ref, gs_ref, cot_ref, norm_ref,
    xs, nall, w, st_part, st_part_in, st_all, own, sendb, recvb,
    g_part, g_part_in, g_all, slope, nb,
    w_sem, c_sem, z_ss, y_ss, core_ss, x_rs,
    stp_ss, stp_rs, st_ss, st_rs, cot_ss, cot_rs, pre_ss, pre_rs,
    gp_ss, gp_rs, g_ss, g_rs, nb_ss, nb_rs,
):
    n, m, lines, width_all, token_count = cfg
    rows, depth = tok_ref.shape
    cot_rows, cols = cot_hbm.shape
    chunks, _, chunk = own.shape
    cores = 2
    per_line = n // (lines * cores)
    scale = 1.0 / math.sqrt(token_count)
    me = lax.axis_index("dp")
    my_mp = lax.axis_index("mp")
    core = lax.rem(me, cores)
    across = lax.rem(me // cores, per_line)
    along = me // (cores * per_line)

    def index(a, b, c):
        return (a * per_line + b) * cores + c

    def dp_peer(k):
        return lax.rem(me + k, n)

    def mp_peer(k):
        return lax.rem(my_mp + k, m)

    w_copy = pltpu.make_async_copy(w_hbm, w, w_sem)
    w_copy.start()
    cot_dst = cot_ref.at[pl.ds(pl.multiple_of(my_mp * cot_rows, cot_rows), cot_rows)]
    cot_copy = pltpu.make_async_copy(cot_hbm, cot_dst, c_sem)
    cot_copy.start()

    barrier = pltpu.get_barrier_semaphore()

    @pl.loop(1, n)
    def _(k):
        pl.semaphore_signal(barrier, inc=1, device_id={"dp": dp_peer(k)}, device_id_type=MESH)

    @pl.loop(1, m)
    def _(k):
        pl.semaphore_signal(barrier, inc=1, device_id={"mp": mp_peer(k)}, device_id_type=MESH)

    values = tok_ref[...].astype(F32)
    lane = lax.broadcasted_iota(jnp.int32, (rows, 128), 1)
    sums = jnp.sum(values, axis=1, keepdims=True)
    squares = jnp.sum(values * values, axis=1, keepdims=True)
    st_part[...] = jnp.where(lane == 0, sums, squares)
    xs[me] = tok_ref[...]

    pl.semaphore_wait(barrier, n + m - 2)

    def line_copy(k):
        return remote(tok_ref, xs.at[me], z_ss.at[k], x_rs.at[me],
                      {"dp": index(lax.rem(along + k, lines), across, core)})

    def across_copy(k, j):
        src = index(lax.rem(along + k, lines), across, core)
        to = index(along, lax.rem(across + j, per_line), core)
        return remote(xs.at[src], xs.at[src], y_ss.at[k, j], x_rs.at[src], {"dp": to})

    def core_copy(k, j):
        src = index(lax.rem(along + k, lines), lax.rem(across + j, per_line), core)
        return remote(xs.at[src], xs.at[src], core_ss.at[k, j], x_rs.at[src],
                      {"dp": index(along, across, 1 - core)})

    def arrived(src):
        remote(xs.at[src], xs.at[src], z_ss.at[0], x_rs.at[src], {"dp": dp_peer(1)}).wait_recv()

    def stp_copy(k):
        return remote(st_part, st_part_in.at[my_mp], stp_ss.at[k], stp_rs.at[my_mp],
                      {"mp": mp_peer(k)})

    def cot_send(k):
        return remote(cot_hbm, cot_dst, cot_ss.at[k], cot_rs.at[my_mp], {"mp": mp_peer(k)})

    for k in range(1, m):
        stp_copy(k).start()
    for k in range(1, lines):
        line_copy(k).start()
    for j in range(1, per_line):
        across_copy(0, j).start()
    core_copy(0, 0).start()

    total = st_part[...]
    for k in range(1, m):
        p = mp_peer(k)
        remote(st_part, st_part_in.at[p], stp_ss.at[0], stp_rs.at[p], {"mp": p}).wait_recv()
        total = total + st_part_in[p]
    for k in range(1, m):
        cot_send(k).start()
    mean = total[:, 0:1] / width_all
    var = total[:, 1:2] / width_all - mean * mean
    st_all[me] = jnp.where(lane == 0, mean, lax.rsqrt(var + 1e-06))

    def st_copy(k):
        return remote(st_all.at[me], st_all.at[me], st_ss.at[k], st_rs.at[me],
                      {"dp": dp_peer(k)})

    @pl.loop(1, n)
    def _(k):
        st_copy(k).start()

    for k in range(1, lines):
        arrived(index(lax.rem(along + k, lines), across, core))
        for j in range(1, per_line):
            across_copy(k, j).start()
        core_copy(k, 0).start()

    @pl.loop(1, n)
    def _(k):
        p = dp_peer(k)
        remote(st_all.at[p], st_all.at[p], st_ss.at[0], st_rs.at[p], {"dp": p}).wait_recv()

    def normalize(src):
        x = xs[src].astype(F32)
        st = st_all[src]
        value = (x - st[:, 0:1]) * st[:, 1:2] * gain_ref[...]
        nall[pl.ds(pl.multiple_of(src * rows, rows), rows), :] = value.astype(BF16)

    @pl.loop(0, lines)
    def _(k):
        normalize(index(lax.rem(along + k, lines), across, core))

    for k in range(lines):
        for j in range(1, per_line):
            arrived(index(lax.rem(along + k, lines), lax.rem(across + j, per_line), core))
            core_copy(k, j).start()

    @pl.loop(0, lines * (per_line - 1))
    def _(i):
        k = i // (per_line - 1)
        j = 1 + lax.rem(i, per_line - 1)
        normalize(index(lax.rem(along + k, lines), lax.rem(across + j, per_line), core))

    @pl.loop(0, lines * per_line)
    def _(i):
        k = i // per_line
        j = lax.rem(i, per_line)
        src = index(lax.rem(along + k, lines), lax.rem(across + j, per_line), 1 - core)
        arrived(src)
        normalize(src)

    w_copy.wait()

    def pre_copy(i, k):
        return remote(sendb.at[i], recvb.at[my_mp, i], pre_ss.at[i, k], pre_rs.at[my_mp, i],
                      {"mp": mp_peer(k)})

    @pl.loop(0, chunks)
    def _(i):
        off = pl.multiple_of(i * chunk, chunk)
        part = jnp.dot(nall[...], w[:, pl.ds(off, chunk)], preferred_element_type=F32)
        own[i] = part
        sendb[i] = part.astype(BF16)
        for k in range(1, m):
            pre_copy(i, k).start()

    mine = pl.ds(pl.multiple_of(me * rows, rows), rows)
    g_part[...] = lax.dot_general(
        nall[mine, :], nall[...], (((1,), (1,)), ((), ())), preferred_element_type=F32
    )

    def gp_copy(k):
        return remote(g_part, g_part_in.at[my_mp], gp_ss.at[k], gp_rs.at[my_mp],
                      {"mp": mp_peer(k)})

    def g_copy(k):
        return remote(g_all.at[mine], g_all.at[mine], g_ss.at[k], g_rs.at[me],
                      {"dp": dp_peer(k)})

    for k in range(1, m):
        gp_copy(k).start()

    @pl.loop(0, depth // 256)
    def _(i):
        off = pl.multiple_of(i * 256, 256)
        nt_ref[pl.ds(off, 256), :] = nall[:, pl.ds(off, 256)].T

    gram = g_part[...]
    for k in range(1, m):
        p = mp_peer(k)
        remote(g_part, g_part_in.at[p], gp_ss.at[0], gp_rs.at[p], {"mp": p}).wait_recv()
        gram = gram + g_part_in[p]
    g_all[mine, :] = gram

    @pl.loop(1, n)
    def _(k):
        g_copy(k).start()

    cot_copy.wait()
    for k in range(1, m):
        p = mp_peer(k)
        dst = cot_ref.at[pl.ds(pl.multiple_of(p * cot_rows, cot_rows), cot_rows)]
        remote(cot_hbm, dst, cot_ss.at[0], cot_rs.at[p], {"mp": p}).wait_recv()

    @pl.loop(1, n)
    def _(k):
        p = dp_peer(k)
        dst = g_all.at[pl.ds(pl.multiple_of(p * rows, rows), rows)]
        remote(dst, dst, g_ss.at[0], g_rs.at[p], {"dp": p}).wait_recv()

    nb[me] = jnp.zeros_like(nb[me])

    @pl.loop(0, chunks)
    def _(i):
        off = pl.multiple_of(i * chunk, chunk)
        pre = own[i]
        for k in range(1, m):
            p = mp_peer(k)
            remote(sendb.at[i], recvb.at[p, i], pre_ss.at[i, 0], pre_rs.at[p, i],
                   {"mp": p}).wait_recv()
            pre = pre + recvb[p, i].astype(F32)
        pre_ref[:, pl.ds(off, chunk)] = pre
        cot = cot_ref[:, pl.ds(off, chunk)].astype(F32)
        slope[...] = (cot * gelu_slope(pre) * scale).astype(BF16)
        gram = g_all[...]
        high = gram.astype(BF16)
        rest = gram - high.astype(F32)
        mid = rest.astype(BF16)
        low = (rest - mid.astype(F32)).astype(BF16)
        s = slope[...]
        gs = (
            jnp.dot(low, s, preferred_element_type=F32)
            + jnp.dot(mid, s, preferred_element_type=F32)
            + jnp.dot(high, s, preferred_element_type=F32)
        )
        gs_ref[:, pl.ds(off, chunk)] = gs
        nb[me] += jnp.full((8, 128), jnp.sum(gs * s.astype(F32)), F32)

    def nb_copy(k):
        return remote(nb.at[me], nb.at[me], nb_ss.at[k], nb_rs.at[me], {"dp": dp_peer(k)})

    @pl.loop(1, n)
    def _(k):
        nb_copy(k).start()

    @pl.loop(1, n)
    def _(k):
        st_copy(k).wait_send()
        g_copy(k).wait_send()

    for k in range(1, lines):
        line_copy(k).wait_send()
    for k in range(lines):
        for j in range(per_line):
            core_copy(k, j).wait_send()
            if j > 0:
                across_copy(k, j).wait_send()
    for k in range(1, m):
        stp_copy(k).wait_send()
        cot_send(k).wait_send()
        gp_copy(k).wait_send()

        @pl.loop(0, chunks)
        def _(i):
            pre_copy(i, k).wait_send()

    @pl.loop(1, n)
    def _(k):
        p = dp_peer(k)
        remote(nb.at[p], nb.at[p], nb_ss.at[0], nb_rs.at[p], {"dp": p}).wait_recv()
        nb_copy(k).wait_send()

    norm_ref[...] = jnp.sum(nb[...], axis=0)


def grad_kernel(token_count, norm_ref, nt_ref, pre_ref, gs_ref, cot_ref, out_ref):
    scale = 1.0 / math.sqrt(token_count)
    size = jnp.sqrt(jnp.maximum(norm_ref[0:1, 0:1], 0.0)) + 1e-12
    radius = 0.5 * math.sqrt(FF)
    pre = pre_ref[...] + radius * gs_ref[...] / size
    slope = (cot_ref[...].astype(F32) * gelu_slope(pre) * scale).astype(BF16)
    out_ref[...] = jnp.dot(nt_ref[...], slope, preferred_element_type=F32)


def per_device(tokens, norm_gain, w_up, cotangent):
    n, m = lax.axis_size("dp"), lax.axis_size("mp")
    rows, depth = tokens.shape
    count = rows * n
    cols = w_up.shape[1]
    lines = 4
    chunk = 256 if cols % 256 == 0 else 128
    chunks = cols // chunk
    per_line = n // (2 * lines)
    cot_rows = cotangent.shape[0]
    dma, vmem = pltpu.SemaphoreType.DMA, pltpu.VMEM
    whole = pl.BlockSpec(memory_space=pltpu.VMEM)
    hbm = pl.BlockSpec(memory_space=pl.ANY)
    cfg = (n, m, lines, depth * m, count)
    nt, pre, gs, cot, norm = pl.pallas_call(
        functools.partial(slopes_kernel, cfg),
        out_shape=(
            jax.ShapeDtypeStruct((depth, count), BF16),
            jax.ShapeDtypeStruct((count, cols), F32),
            jax.ShapeDtypeStruct((count, cols), F32),
            jax.ShapeDtypeStruct((count, cols), BF16),
            jax.ShapeDtypeStruct((8, 128), F32),
        ),
        in_specs=[whole, whole, hbm, hbm],
        out_specs=[whole] * 5,
        scratch_shapes=[
            vmem((n, rows, depth), BF16),
            vmem((count, depth), BF16),
            vmem((depth, cols), BF16),
            vmem((rows, 128), F32),
            vmem((m, rows, 128), F32),
            vmem((n, rows, 128), F32),
            vmem((chunks, count, chunk), F32),
            vmem((chunks, count, chunk), BF16),
            vmem((m, chunks, count, chunk), BF16),
            vmem((rows, count), F32),
            vmem((m, rows, count), F32),
            vmem((count, count), F32),
            vmem((count, chunk), BF16),
            vmem((n, 8, 128), F32),
            dma(()), dma(()), dma((lines,)), dma((lines, per_line)), dma((lines, per_line)),
            dma((n,)),
            dma((m,)), dma((m,)), dma((n,)), dma((n,)), dma((m,)), dma((m,)),
            dma((chunks, m)), dma((m, chunks)),
            dma((m,)), dma((m,)), dma((n,)), dma((n,)), dma((n,)), dma((n,)),
        ],
        compiler_params=pltpu.CompilerParams(
            collective_id=0, has_side_effects=True, vmem_limit_bytes=56 * 2**20
        ),
        name="slopes",
    )(tokens, norm_gain.reshape(1, depth), w_up, cotangent)

    return pl.pallas_call(
        functools.partial(grad_kernel, count),
        grid=(chunks,),
        out_shape=jax.ShapeDtypeStruct((depth, cols), F32),
        in_specs=[
            pl.BlockSpec((8, 128), lambda i: (0, 0)),
            pl.BlockSpec((depth, count), lambda i: (0, 0)),
            pl.BlockSpec((count, chunk), lambda i: (0, i)),
            pl.BlockSpec((count, chunk), lambda i: (0, i)),
            pl.BlockSpec((count, chunk), lambda i: (0, i)),
        ],
        out_specs=pl.BlockSpec((depth, chunk), lambda i: (0, i)),
        compiler_params=pltpu.CompilerParams(vmem_limit_bytes=40 * 2**20),
        name="grad",
    )(norm, nt, pre, gs, cot)


def solution(mesh):
    placed = (P("dp", "mp"), P("mp"), P("mp", "dp"), P("mp", "dp"))
    return jax.shard_map(
        per_device, mesh=mesh, in_specs=placed, out_specs=P("mp", "dp"), check_vma=False
    )
```

```python
import functools
import math

import jax
import jax.numpy as jnp
from jax import lax
from jax.experimental import pallas as pl
from jax.experimental.pallas import tpu as pltpu
from jax.sharding import PartitionSpec as P

FF = 24576
MESH = pl.DeviceIdType.MESH
F32 = jnp.float32
BF16 = jnp.bfloat16


def gelu_slope(value):
    cdf = 0.5 * (1.0 + lax.erf(value * (1.0 / math.sqrt(2.0))))
    dens = jnp.exp(-0.5 * value * value) * (1.0 / math.sqrt(2.0 * math.pi))
    return cdf + value * dens


def remote(src, dst, send_sem, recv_sem, device):
    return pltpu.make_async_remote_copy(
        src_ref=src, dst_ref=dst, send_sem=send_sem, recv_sem=recv_sem,
        device_id=device, device_id_type=MESH,
    )


def slopes_kernel(
    cfg,
    tok_ref, gain_ref, w_hbm, cot_hbm,
    nt_hbm, pre_hbm, gs_hbm, cot_out, norm_ref,
    nt_ref, pre_ref, gs_ref, cot_ref, g_terms,
    xs, nall, w, st_part, st_part_in, st_all, own, sendb, recvb,
    g_part, g_part_in, g_all, slope, nb,
    w_sem, c_sem, o_sem, pre_os, gs_os, z_ss, y_ss, core_ss, x_rs,
    stp_ss, stp_rs, st_ss, st_rs, cot_ss, cot_rs, pre_ss, pre_rs,
    gp_ss, gp_rs, g_ss, g_rs, nb_ss, nb_rs,
):
    n, m, lines, width_all, token_count = cfg
    rows, depth = tok_ref.shape
    cot_rows, cols = cot_hbm.shape
    chunks, _, chunk = own.shape
    cores = 2
    per_line = n // (lines * cores)
    scale = 1.0 / math.sqrt(token_count)
    me = lax.axis_index("dp")
    my_mp = lax.axis_index("mp")
    core = lax.rem(me, cores)
    across = lax.rem(me // cores, per_line)
    along = me // (cores * per_line)

    def index(a, b, c):
        return (a * per_line + b) * cores + c

    def dp_peer(k):
        return lax.rem(me + k, n)

    def mp_peer(k):
        return lax.rem(my_mp + k, m)

    w_copy = pltpu.make_async_copy(w_hbm, w, w_sem)
    w_copy.start()
    cot_dst = cot_ref.at[pl.ds(pl.multiple_of(my_mp * cot_rows, cot_rows), cot_rows)]
    cot_copy = pltpu.make_async_copy(cot_hbm, cot_dst, c_sem)
    cot_copy.start()

    barrier = pltpu.get_barrier_semaphore()

    @pl.loop(1, n)
    def _(k):
        pl.semaphore_signal(barrier, inc=1, device_id={"dp": dp_peer(k)}, device_id_type=MESH)

    @pl.loop(1, m)
    def _(k):
        pl.semaphore_signal(barrier, inc=1, device_id={"mp": mp_peer(k)}, device_id_type=MESH)

    values = tok_ref[...].astype(F32)
    lane = lax.broadcasted_iota(jnp.int32, (rows, 128), 1)
    sums = jnp.sum(values, axis=1, keepdims=True)
    squares = jnp.sum(values * values, axis=1, keepdims=True)
    st_part[...] = jnp.where(lane == 0, sums, squares)
    xs[me] = tok_ref[...]

    pl.semaphore_wait(barrier, n + m - 2)

    def line_copy(src_a, up):
        src = index(src_a, across, core)
        to = index(along + 1 if up else along - 1, across, core)
        return remote(xs.at[src], xs.at[src], z_ss.at[int(up), src_a], x_rs.at[src], {"dp": to})

    def across_copy(src_a, j):
        src = index(src_a, across, core)
        to = index(along, lax.rem(across + j, per_line), core)
        return remote(xs.at[src], xs.at[src], y_ss.at[src_a, j], x_rs.at[src], {"dp": to})

    def core_copy(src_a, j):
        src = index(src_a, lax.rem(across + j, per_line), core)
        return remote(xs.at[src], xs.at[src], core_ss.at[src_a, j], x_rs.at[src],
                      {"dp": index(along, across, 1 - core)})

    def arrived(src):
        remote(xs.at[src], xs.at[src], z_ss.at[0, 0], x_rs.at[src], {"dp": dp_peer(1)}).wait_recv()

    by_distance = [(along - s if low else along + s, low) for s in range(1, lines) for low in (True, False)]

    def there(pos, low):
        return pos >= 0 if low else pos < lines

    def can_go(up):
        return along + 1 < lines if up else along > 0

    def across_step(pos):
        for j in range(1, per_line):
            arrived(index(pos, lax.rem(across + j, per_line), core))
            core_copy(pos, j).start()

    def stp_copy(k):
        return remote(st_part, st_part_in.at[my_mp], stp_ss.at[k], stp_rs.at[my_mp],
                      {"mp": mp_peer(k)})

    def cot_send(k):
        return remote(cot_hbm, cot_dst, cot_ss.at[k], cot_rs.at[my_mp], {"mp": mp_peer(k)})

    for k in range(1, m):
        stp_copy(k).start()
    for up in (True, False):
        @pl.when(can_go(up))
        def _():
            line_copy(along, up).start()
    for j in range(1, per_line):
        across_copy(along, j).start()
    core_copy(along, 0).start()

    total = st_part[...]
    for k in range(1, m):
        p = mp_peer(k)
        remote(st_part, st_part_in.at[p], stp_ss.at[0], stp_rs.at[p], {"mp": p}).wait_recv()
        total = total + st_part_in[p]
    for k in range(1, m):
        cot_send(k).start()
    mean = total[:, 0:1] / width_all
    var = total[:, 1:2] / width_all - mean * mean
    st_all[me] = jnp.where(lane == 0, mean, lax.rsqrt(var + 1e-06))

    def st_copy(k):
        return remote(st_all.at[me], st_all.at[me], st_ss.at[k], st_rs.at[me],
                      {"dp": dp_peer(k)})

    @pl.loop(1, n)
    def _(k):
        st_copy(k).start()

    for pos, low in by_distance:
        @pl.when(there(pos, low))
        def _():
            arrived(index(pos, across, core))

            @pl.when(can_go(low))
            def _():
                line_copy(pos, low).start()

            for j in range(1, per_line):
                across_copy(pos, j).start()
            core_copy(pos, 0).start()

    @pl.loop(1, n)
    def _(k):
        p = dp_peer(k)
        remote(st_all.at[p], st_all.at[p], st_ss.at[0], st_rs.at[p], {"dp": p}).wait_recv()

    def normalize(src):
        x = xs[src].astype(F32)
        st = st_all[src]
        value = (x - st[:, 0:1]) * st[:, 1:2] * gain_ref[...]
        nall[pl.ds(pl.multiple_of(src * rows, rows), rows), :] = value.astype(BF16)

    @pl.loop(0, lines)
    def _(k):
        normalize(index(lax.rem(along + k, lines), across, core))

    across_step(along)
    for pos, low in by_distance:
        @pl.when(there(pos, low))
        def _():
            across_step(pos)

    @pl.loop(0, lines * (per_line - 1))
    def _(i):
        k = i // (per_line - 1)
        j = 1 + lax.rem(i, per_line - 1)
        normalize(index(lax.rem(along + k, lines), lax.rem(across + j, per_line), core))

    @pl.loop(0, lines * per_line)
    def _(i):
        k = i // per_line
        j = lax.rem(i, per_line)
        src = index(lax.rem(along + k, lines), lax.rem(across + j, per_line), 1 - core)
        arrived(src)
        normalize(src)

    w_copy.wait()

    def pre_copy(i, k):
        return remote(sendb.at[i], recvb.at[my_mp, i], pre_ss.at[i, k], pre_rs.at[my_mp, i],
                      {"mp": mp_peer(k)})

    def project(i):
        off = pl.multiple_of(i * chunk, chunk)
        part = jnp.dot(nall[...], w[:, pl.ds(off, chunk)], preferred_element_type=F32)
        own[i] = part
        sendb[i] = part.astype(BF16)
        for k in range(1, m):
            pre_copy(i, k).start()

    project(0)

    mine = pl.ds(pl.multiple_of(me * rows, rows), rows)
    g_part[...] = lax.dot_general(
        nall[mine, :], nall[...], (((1,), (1,)), ((), ())), preferred_element_type=F32
    )

    def gp_copy(k):
        return remote(g_part, g_part_in.at[my_mp], gp_ss.at[k], gp_rs.at[my_mp],
                      {"mp": mp_peer(k)})

    def g_copy(k):
        return remote(g_all.at[mine], g_all.at[mine], g_ss.at[k], g_rs.at[me],
                      {"dp": dp_peer(k)})

    for k in range(1, m):
        gp_copy(k).start()

    @pl.loop(1, chunks)
    def _(i):
        project(i)

    gram = g_part[...]
    for k in range(1, m):
        p = mp_peer(k)
        remote(g_part, g_part_in.at[p], gp_ss.at[0], gp_rs.at[p], {"mp": p}).wait_recv()
        gram = gram + g_part_in[p]
    g_all[mine, :] = gram

    @pl.loop(1, n)
    def _(k):
        g_copy(k).start()

    @pl.loop(0, depth // 256)
    def _(i):
        off = pl.multiple_of(i * 256, 256)
        nt_ref[pl.ds(off, 256), :] = nall[:, pl.ds(off, 256)].T

    nt_copy = pltpu.make_async_copy(nt_ref, nt_hbm, o_sem.at[0])
    nt_copy.start()

    cot_copy.wait()
    for k in range(1, m):
        p = mp_peer(k)
        dst = cot_ref.at[pl.ds(pl.multiple_of(p * cot_rows, cot_rows), cot_rows)]
        remote(cot_hbm, dst, cot_ss.at[0], cot_rs.at[p], {"mp": p}).wait_recv()

    @pl.loop(1, n)
    def _(k):
        p = dp_peer(k)
        dst = g_all.at[pl.ds(pl.multiple_of(p * rows, rows), rows)]
        remote(dst, dst, g_ss.at[0], g_rs.at[p], {"dp": p}).wait_recv()

    cot_write = pltpu.make_async_copy(cot_ref, cot_out, o_sem.at[1])
    cot_write.start()

    rest = g_all[...]
    for t in range(3):
        g_terms[t] = rest.astype(BF16)
        rest = rest - g_terms[t].astype(F32)

    def out_copy(i, buf, dst, sem):
        cut = pl.ds(pl.multiple_of(i * chunk, chunk), chunk)
        return pltpu.make_async_copy(buf.at[:, cut], dst.at[:, cut], sem.at[i])

    nb[me] = jnp.zeros_like(nb[me])

    @pl.loop(0, chunks)
    def _(i):
        off = pl.multiple_of(i * chunk, chunk)
        pre = own[i]
        for k in range(1, m):
            p = mp_peer(k)
            remote(sendb.at[i], recvb.at[p, i], pre_ss.at[i, 0], pre_rs.at[p, i],
                   {"mp": p}).wait_recv()
            pre = pre + recvb[p, i].astype(F32)
        pre_ref[:, pl.ds(off, chunk)] = pre
        cot = cot_ref[:, pl.ds(off, chunk)].astype(F32)
        slope[...] = (cot * gelu_slope(pre) * scale).astype(BF16)
        out_copy(i, pre_ref, pre_hbm, pre_os).start()
        s = slope[...]
        gs = (
            jnp.dot(g_terms[2], s, preferred_element_type=F32)
            + jnp.dot(g_terms[1], s, preferred_element_type=F32)
            + jnp.dot(g_terms[0], s, preferred_element_type=F32)
        )
        gs_ref[:, pl.ds(off, chunk)] = gs
        out_copy(i, gs_ref, gs_hbm, gs_os).start()
        nb[me] += jnp.full((8, 128), jnp.sum(gs * s.astype(F32)), F32)

    def nb_copy(k):
        return remote(nb.at[me], nb.at[me], nb_ss.at[k], nb_rs.at[me], {"dp": dp_peer(k)})

    @pl.loop(1, n)
    def _(k):
        nb_copy(k).start()

    @pl.loop(1, n)
    def _(k):
        st_copy(k).wait_send()
        g_copy(k).wait_send()

    for pos, low in [(along, True), (along, False)] + by_distance:
        @pl.when(jnp.logical_and(there(pos, low), can_go(low)))
        def _():
            line_copy(pos, low).wait_send()

    @pl.loop(0, lines)
    def _(pos):
        for j in range(per_line):
            core_copy(pos, j).wait_send()
            if j > 0:
                across_copy(pos, j).wait_send()

    nt_copy.wait()
    cot_write.wait()

    @pl.loop(0, chunks)
    def _(i):
        out_copy(i, pre_ref, pre_hbm, pre_os).wait()
        out_copy(i, gs_ref, gs_hbm, gs_os).wait()

    for k in range(1, m):
        stp_copy(k).wait_send()
        cot_send(k).wait_send()
        gp_copy(k).wait_send()

        @pl.loop(0, chunks)
        def _(i):
            pre_copy(i, k).wait_send()

    @pl.loop(1, n)
    def _(k):
        p = dp_peer(k)
        remote(nb.at[p], nb.at[p], nb_ss.at[0], nb_rs.at[p], {"dp": p}).wait_recv()
        nb_copy(k).wait_send()

    norm_ref[...] = jnp.sum(nb[...], axis=0)


def grad_kernel(token_count, norm_ref, nt_ref, pre_ref, gs_ref, cot_ref, out_ref, slope_ref):
    @pl.when(pl.program_id(0) == 0)
    def _():
        slope_ref[...] = jnp.zeros_like(slope_ref)

    before = slope_ref[...]
    scale = 1.0 / math.sqrt(token_count)
    size = jnp.sqrt(jnp.maximum(norm_ref[0:1, 0:1], 0.0)) + 1e-12
    radius = 0.5 * math.sqrt(FF)
    pre = pre_ref[...] + radius * gs_ref[...] / size
    out_ref[...] = jnp.dot(nt_ref[...], before, preferred_element_type=F32)
    slope_ref[...] = (cot_ref[...].astype(F32) * gelu_slope(pre) * scale).astype(BF16)


def per_device(tokens, norm_gain, w_up, cotangent):
    n, m = lax.axis_size("dp"), lax.axis_size("mp")
    rows, depth = tokens.shape
    count = rows * n
    cols = w_up.shape[1]
    lines = 4
    chunk = 256 if cols % 256 == 0 else 128
    chunks = cols // chunk
    per_line = n // (2 * lines)
    cot_rows = cotangent.shape[0]
    dma, vmem = pltpu.SemaphoreType.DMA, pltpu.VMEM
    whole = pl.BlockSpec(memory_space=pltpu.VMEM)
    hbm = pl.BlockSpec(memory_space=pl.ANY)
    cfg = (n, m, lines, depth * m, count)
    nt, pre, gs, cot, norm = pl.pallas_call(
        functools.partial(slopes_kernel, cfg),
        out_shape=(
            jax.ShapeDtypeStruct((depth, count), BF16),
            jax.ShapeDtypeStruct((count, cols), F32),
            jax.ShapeDtypeStruct((count, cols), F32),
            jax.ShapeDtypeStruct((count, cols), BF16),
            jax.ShapeDtypeStruct((8, 128), F32),
        ),
        in_specs=[whole, whole, hbm, hbm],
        out_specs=[hbm] * 4 + [whole],
        scratch_shapes=[
            vmem((depth, count), BF16),
            vmem((count, cols), F32),
            vmem((count, cols), F32),
            vmem((count, cols), BF16),
            vmem((3, count, count), BF16),
            vmem((n, rows, depth), BF16),
            vmem((count, depth), BF16),
            vmem((depth, cols), BF16),
            vmem((rows, 128), F32),
            vmem((m, rows, 128), F32),
            vmem((n, rows, 128), F32),
            vmem((chunks, count, chunk), F32),
            vmem((chunks, count, chunk), BF16),
            vmem((m, chunks, count, chunk), BF16),
            vmem((rows, count), F32),
            vmem((m, rows, count), F32),
            vmem((count, count), F32),
            vmem((count, chunk), BF16),
            vmem((n, 8, 128), F32),
            dma(()), dma(()), dma((2,)), dma((chunks,)), dma((chunks,)),
            dma((2, lines)), dma((lines, per_line)), dma((lines, per_line)),
            dma((n,)),
            dma((m,)), dma((m,)), dma((n,)), dma((n,)), dma((m,)), dma((m,)),
            dma((chunks, m)), dma((m, chunks)),
            dma((m,)), dma((m,)), dma((n,)), dma((n,)), dma((n,)), dma((n,)),
        ],
        compiler_params=pltpu.CompilerParams(
            collective_id=0, has_side_effects=True, vmem_limit_bytes=56 * 2**20
        ),
        name="slopes",
    )(tokens, norm_gain.reshape(1, depth), w_up, cotangent)

    return pl.pallas_call(
        functools.partial(grad_kernel, count),
        grid=(chunks + 1,),
        out_shape=jax.ShapeDtypeStruct((depth, cols), F32),
        in_specs=[
            pl.BlockSpec((8, 128), lambda i: (0, 0)),
            pl.BlockSpec((depth, count), lambda i: (0, 0)),
            pl.BlockSpec((count, chunk), lambda i: (0, jnp.minimum(i, chunks - 1))),
            pl.BlockSpec((count, chunk), lambda i: (0, jnp.minimum(i, chunks - 1))),
            pl.BlockSpec((count, chunk), lambda i: (0, jnp.minimum(i, chunks - 1))),
        ],
        out_specs=pl.BlockSpec((depth, chunk), lambda i: (0, jnp.maximum(i - 1, 0))),
        scratch_shapes=[vmem((count, chunk), BF16)],
        compiler_params=pltpu.CompilerParams(vmem_limit_bytes=60 * 2**20),
        name="grad",
    )(norm, nt, pre, gs, cot)


def solution(mesh):
    placed = (P("dp", "mp"), P("mp"), P("mp", "dp"), P("mp", "dp"))
    return jax.shard_map(
        per_device, mesh=mesh, in_specs=placed, out_specs=P("mp", "dp"), check_vma=False
    )
```

```python
import functools
import math

import jax
import jax.numpy as jnp
from jax import lax
from jax.experimental import pallas as pl
from jax.experimental.pallas import tpu as pltpu
from jax.sharding import PartitionSpec as P

FF = 24576
MESH = pl.DeviceIdType.MESH
F32 = jnp.float32
BF16 = jnp.bfloat16


def gelu_slope(value):
    cdf = 0.5 * (1.0 + lax.erf(value * (1.0 / math.sqrt(2.0))))
    dens = jnp.exp(-0.5 * value * value) * (1.0 / math.sqrt(2.0 * math.pi))
    return cdf + value * dens


def remote(src, dst, send_sem, recv_sem, device):
    return pltpu.make_async_remote_copy(
        src_ref=src, dst_ref=dst, send_sem=send_sem, recv_sem=recv_sem,
        device_id=device, device_id_type=MESH,
    )


def slopes_kernel(
    cfg,
    tok_ref, gain_ref, w_hbm, cot_hbm,
    nt_hbm, slope_hbm,
    nt_ref, pre_ref, gs_ref, cot_ref, g_terms, nlocal,
    xs, nall, w, st_part, st_part_in, st_all, own, sendb, recvb,
    g_part, g_part_in, g_all, slope, nb,
    w_sem, c_sem, o_sem, slope_os, z_ss, y_ss, core_ss, x_rs,
    stp_ss, stp_rs, st_ss, st_rs, cot_ss, cot_rs, pre_ss, pre_rs,
    gp_ss, gp_rs, g_ss, g_rs, nb_ss, nb_rs,
):
    n, m, lines, width_all, token_count = cfg
    rows, depth = tok_ref.shape
    cot_rows, cols = cot_hbm.shape
    chunks, _, chunk = own.shape
    cores = 2
    per_line = n // (lines * cores)
    scale = 1.0 / math.sqrt(token_count)
    me = lax.axis_index("dp")
    my_mp = lax.axis_index("mp")
    core = lax.rem(me, cores)
    across = lax.rem(me // cores, per_line)
    along = me // (cores * per_line)

    group = rows * cores
    near = lines * group
    parts = [(0, near), (near, token_count - near)]

    def index(a, b, c):
        return (a * per_line + b) * cores + c

    def dp_peer(k):
        return lax.rem(me + k, n)

    def mp_peer(k):
        return lax.rem(my_mp + k, m)

    w_copy = pltpu.make_async_copy(w_hbm, w, w_sem)
    w_copy.start()
    cot_dst = cot_ref.at[pl.ds(pl.multiple_of(my_mp * cot_rows, cot_rows), cot_rows)]
    cot_copy = pltpu.make_async_copy(cot_hbm, cot_dst, c_sem)
    cot_copy.start()

    barrier = pltpu.get_barrier_semaphore()

    @pl.loop(1, n)
    def _(k):
        pl.semaphore_signal(barrier, inc=1, device_id={"dp": dp_peer(k)}, device_id_type=MESH)

    @pl.loop(1, m)
    def _(k):
        pl.semaphore_signal(barrier, inc=1, device_id={"mp": mp_peer(k)}, device_id_type=MESH)

    values = tok_ref[...].astype(F32)
    lane = lax.broadcasted_iota(jnp.int32, (rows, 128), 1)
    sums = jnp.sum(values, axis=1, keepdims=True)
    squares = jnp.sum(values * values, axis=1, keepdims=True)
    st_part[...] = jnp.where(lane == 0, sums, squares)
    xs[me] = tok_ref[...]

    pl.semaphore_wait(barrier, n + m - 2)

    def line_copy(src_a, up):
        src = index(src_a, across, core)
        to = index(along + 1 if up else along - 1, across, core)
        return remote(xs.at[src], xs.at[src], z_ss.at[int(up), src_a], x_rs.at[src], {"dp": to})

    def across_copy(src_a, j):
        src = index(src_a, across, core)
        to = index(along, lax.rem(across + j, per_line), core)
        return remote(xs.at[src], xs.at[src], y_ss.at[src_a, j], x_rs.at[src], {"dp": to})

    def core_copy(src_a, j):
        src = index(src_a, lax.rem(across + j, per_line), core)
        return remote(xs.at[src], xs.at[src], core_ss.at[src_a, j], x_rs.at[src],
                      {"dp": index(along, across, 1 - core)})

    def arrived(src):
        remote(xs.at[src], xs.at[src], z_ss.at[0, 0], x_rs.at[src], {"dp": dp_peer(1)}).wait_recv()

    by_distance = [(along - s if low else along + s, low) for s in range(1, lines) for low in (True, False)]

    def there(pos, low):
        return pos >= 0 if low else pos < lines

    def can_go(up):
        return along + 1 < lines if up else along > 0

    def across_step(pos):
        for j in range(1, per_line):
            arrived(index(pos, lax.rem(across + j, per_line), core))
            core_copy(pos, j).start()

    def stp_copy(k):
        return remote(st_part, st_part_in.at[my_mp], stp_ss.at[k], stp_rs.at[my_mp],
                      {"mp": mp_peer(k)})

    def cot_send(k):
        return remote(cot_hbm, cot_dst, cot_ss.at[k], cot_rs.at[my_mp], {"mp": mp_peer(k)})

    for k in range(1, m):
        stp_copy(k).start()
    for up in (True, False):
        @pl.when(can_go(up))
        def _():
            line_copy(along, up).start()
    for j in range(1, per_line):
        across_copy(along, j).start()
    core_copy(along, 0).start()

    total = st_part[...]
    for k in range(1, m):
        p = mp_peer(k)
        remote(st_part, st_part_in.at[p], stp_ss.at[0], stp_rs.at[p], {"mp": p}).wait_recv()
        total = total + st_part_in[p]
    for k in range(1, m):
        cot_send(k).start()
    mean = total[:, 0:1] / width_all
    var = total[:, 1:2] / width_all - mean * mean
    st_all[me] = jnp.where(lane == 0, mean, lax.rsqrt(var + 1e-06))

    def st_copy(k):
        return remote(st_all.at[me], st_all.at[me], st_ss.at[k], st_rs.at[me],
                      {"dp": dp_peer(k)})

    @pl.loop(1, n)
    def _(k):
        st_copy(k).start()

    for pos, low in by_distance:
        @pl.when(there(pos, low))
        def _():
            arrived(index(pos, across, core))

            @pl.when(can_go(low))
            def _():
                line_copy(pos, low).start()

            for j in range(1, per_line):
                across_copy(pos, j).start()
            core_copy(pos, 0).start()

    @pl.loop(1, n)
    def _(k):
        p = dp_peer(k)
        remote(st_all.at[p], st_all.at[p], st_ss.at[0], st_rs.at[p], {"dp": p}).wait_recv()

    def normalize(src):
        x = xs[src].astype(F32)
        st = st_all[src]
        value = ((x - st[:, 0:1]) * st[:, 1:2] * gain_ref[...]).astype(BF16)
        nall[pl.ds(pl.multiple_of(src * rows, rows), rows), :] = value
        a = src // (cores * per_line)
        p = lax.rem(lax.rem(src // cores, per_line) + per_line - across, per_line)
        local = ((p * lines + a) * cores + lax.rem(src, cores)) * rows
        nlocal[pl.ds(pl.multiple_of(local, rows), rows), :] = value

    @pl.loop(0, lines)
    def _(k):
        normalize(index(lax.rem(along + k, lines), across, core))

    @pl.loop(0, lines)
    def _(k):
        src = index(lax.rem(along + k, lines), across, 1 - core)
        arrived(src)
        normalize(src)

    w_copy.wait()

    def pre_copy(part, i, k):
        at, size = parts[part]
        return remote(sendb.at[i, pl.ds(at, size)], recvb.at[my_mp, i, pl.ds(at, size)],
                      pre_ss.at[part, i, k], pre_rs.at[part, my_mp, i], {"mp": mp_peer(k)})

    def project(part, i):
        at, size = parts[part]
        off = pl.multiple_of(i * chunk, chunk)
        value = jnp.dot(nlocal[pl.ds(at, size), :], w[:, pl.ds(off, chunk)],
                        preferred_element_type=F32)
        own[i, pl.ds(at, size)] = value
        sendb[i, pl.ds(at, size)] = value.astype(BF16)
        for k in range(1, m):
            pre_copy(part, i, k).start()

    first = min(2, chunks)

    @pl.loop(0, first)
    def _(i):
        project(0, i)

    across_step(along)
    for pos, low in by_distance:
        @pl.when(there(pos, low))
        def _():
            across_step(pos)

    @pl.loop(first, chunks)
    def _(i):
        project(0, i)

    @pl.loop(0, lines * (per_line - 1))
    def _(i):
        k = i // (per_line - 1)
        j = 1 + lax.rem(i, per_line - 1)
        normalize(index(lax.rem(along + k, lines), lax.rem(across + j, per_line), core))

    @pl.loop(0, lines * (per_line - 1))
    def _(i):
        k = i // (per_line - 1)
        j = 1 + lax.rem(i, per_line - 1)
        src = index(lax.rem(along + k, lines), lax.rem(across + j, per_line), 1 - core)
        arrived(src)
        normalize(src)

    mine = pl.ds(pl.multiple_of(me * rows, rows), rows)
    g_part[...] = lax.dot_general(
        nall[mine, :], nall[...], (((1,), (1,)), ((), ())), preferred_element_type=F32
    )

    def gp_copy(k):
        return remote(g_part, g_part_in.at[my_mp], gp_ss.at[k], gp_rs.at[my_mp],
                      {"mp": mp_peer(k)})

    def g_copy(k):
        return remote(g_all.at[mine], g_all.at[mine], g_ss.at[k], g_rs.at[me],
                      {"dp": dp_peer(k)})

    for k in range(1, m):
        gp_copy(k).start()

    @pl.loop(0, chunks)
    def _(i):
        project(1, i)

    @pl.loop(0, depth // 256)
    def _(i):
        off = pl.multiple_of(i * 256, 256)
        nt_ref[pl.ds(off, 256), :] = nall[:, pl.ds(off, 256)].T

    nt_copy = pltpu.make_async_copy(nt_ref, nt_hbm, o_sem.at[0])
    nt_copy.start()

    cot_copy.wait()
    for k in range(1, m):
        p = mp_peer(k)
        dst = cot_ref.at[pl.ds(pl.multiple_of(p * cot_rows, cot_rows), cot_rows)]
        remote(cot_hbm, dst, cot_ss.at[0], cot_rs.at[p], {"mp": p}).wait_recv()

    def local_groups(part):
        at, size = parts[part]
        for g in range(at // group, (at + size) // group):
            p, a = g // lines, g % lines
            row = (a * per_line + lax.rem(across + p, per_line)) * group
            yield pl.ds(pl.multiple_of(row, group), group)

    def first_slopes(part, i):
        at, size = parts[part]
        off = pl.multiple_of(i * chunk, chunk)
        pre = own[i, pl.ds(at, size)]
        for k in range(1, m):
            p = mp_peer(k)
            remote(sendb.at[i, pl.ds(at, size)], recvb.at[p, i, pl.ds(at, size)],
                   pre_ss.at[part, i, 0], pre_rs.at[part, p, i], {"mp": p}).wait_recv()
            pre = pre + recvb[p, i, pl.ds(at, size)].astype(F32)
        cot = jnp.concatenate([cot_ref[r, pl.ds(off, chunk)] for r in local_groups(part)], axis=0)
        s = (cot.astype(F32) * gelu_slope(pre) * scale).astype(BF16)
        for g, r in enumerate(local_groups(part)):
            pre_ref[r, pl.ds(off, chunk)] = pre[g * group:(g + 1) * group]
            slope[r, pl.ds(off, chunk)] = s[g * group:(g + 1) * group]

    @pl.loop(0, chunks)
    def _(i):
        first_slopes(0, i)

    gram = g_part[...]
    for k in range(1, m):
        p = mp_peer(k)
        remote(g_part, g_part_in.at[p], gp_ss.at[0], gp_rs.at[p], {"mp": p}).wait_recv()
        gram = gram + g_part_in[p]
    g_all[mine, :] = gram

    @pl.loop(1, n)
    def _(k):
        g_copy(k).start()

    @pl.loop(1, n)
    def _(k):
        p = dp_peer(k)
        dst = g_all.at[pl.ds(pl.multiple_of(p * rows, rows), rows)]
        remote(dst, dst, g_ss.at[0], g_rs.at[p], {"dp": p}).wait_recv()

    rest = g_all[...]
    for t in range(3):
        g_terms[t] = rest.astype(BF16)
        rest = rest - g_terms[t].astype(F32)

    nb[me] = jnp.zeros_like(nb[me])

    @pl.loop(0, chunks)
    def _(i):
        first_slopes(1, i)
        off = pl.multiple_of(i * chunk, chunk)
        s = slope[:, pl.ds(off, chunk)]
        gs = (
            jnp.dot(g_terms[2], s, preferred_element_type=F32)
            + jnp.dot(g_terms[1], s, preferred_element_type=F32)
            + jnp.dot(g_terms[0], s, preferred_element_type=F32)
        )
        gs_ref[:, pl.ds(off, chunk)] = gs
        nb[me] += jnp.full((8, 128), jnp.sum(gs * s.astype(F32)), F32)

    def nb_copy(k):
        return remote(nb.at[me], nb.at[me], nb_ss.at[k], nb_rs.at[me], {"dp": dp_peer(k)})

    @pl.loop(1, n)
    def _(k):
        nb_copy(k).start()

    @pl.loop(1, n)
    def _(k):
        st_copy(k).wait_send()
        g_copy(k).wait_send()

    for pos, low in [(along, True), (along, False)] + by_distance:
        @pl.when(jnp.logical_and(there(pos, low), can_go(low)))
        def _():
            line_copy(pos, low).wait_send()

    @pl.loop(0, lines)
    def _(pos):
        for j in range(per_line):
            core_copy(pos, j).wait_send()
            if j > 0:
                across_copy(pos, j).wait_send()

    for k in range(1, m):
        stp_copy(k).wait_send()
        cot_send(k).wait_send()
        gp_copy(k).wait_send()

        @pl.loop(0, chunks)
        def _(i):
            pre_copy(0, i, k).wait_send()
            pre_copy(1, i, k).wait_send()

    @pl.loop(1, n)
    def _(k):
        p = dp_peer(k)
        remote(nb.at[p], nb.at[p], nb_ss.at[0], nb_rs.at[p], {"dp": p}).wait_recv()
        nb_copy(k).wait_send()

    squared = jnp.sum(nb[...], axis=0)[0:1, 0:1]
    size = jnp.sqrt(jnp.maximum(squared, 0.0)) + 1e-12
    radius = 0.5 * math.sqrt(FF)

    def slope_copy(i):
        at = pl.ds(pl.multiple_of(i * chunk, chunk), chunk)
        return pltpu.make_async_copy(slope.at[:, at], slope_hbm.at[:, at], slope_os.at[i])

    @pl.loop(0, chunks)
    def _(i):
        at = pl.ds(pl.multiple_of(i * chunk, chunk), chunk)
        pre = pre_ref[:, at] + radius * gs_ref[:, at] / size
        slope[:, at] = (cot_ref[:, at].astype(F32) * gelu_slope(pre) * scale).astype(BF16)
        slope_copy(i).start()

    nt_copy.wait()

    @pl.loop(0, chunks)
    def _(i):
        slope_copy(i).wait()


def grad_kernel(nt_ref, slope_ref, out_ref):
    out_ref[...] = jnp.dot(nt_ref[...], slope_ref[...], preferred_element_type=F32)


def per_device(tokens, norm_gain, w_up, cotangent):
    n, m = lax.axis_size("dp"), lax.axis_size("mp")
    rows, depth = tokens.shape
    count = rows * n
    cols = w_up.shape[1]
    lines = 4
    chunk = 256 if cols % 256 == 0 else 128
    chunks = cols // chunk
    per_line = n // (2 * lines)
    cot_rows = cotangent.shape[0]
    dma, vmem = pltpu.SemaphoreType.DMA, pltpu.VMEM
    whole = pl.BlockSpec(memory_space=pltpu.VMEM)
    hbm = pl.BlockSpec(memory_space=pl.ANY)
    cfg = (n, m, lines, depth * m, count)
    nt, slope = pl.pallas_call(
        functools.partial(slopes_kernel, cfg),
        out_shape=(
            jax.ShapeDtypeStruct((depth, count), BF16),
            jax.ShapeDtypeStruct((count, cols), BF16),
        ),
        in_specs=[whole, whole, hbm, hbm],
        out_specs=[hbm] * 2,
        scratch_shapes=[
            vmem((depth, count), BF16),
            vmem((count, cols), F32),
            vmem((count, cols), F32),
            vmem((count, cols), BF16),
            vmem((3, count, count), BF16),
            vmem((count, depth), BF16),
            vmem((n, rows, depth), BF16),
            vmem((count, depth), BF16),
            vmem((depth, cols), BF16),
            vmem((rows, 128), F32),
            vmem((m, rows, 128), F32),
            vmem((n, rows, 128), F32),
            vmem((chunks, count, chunk), F32),
            vmem((chunks, count, chunk), BF16),
            vmem((m, chunks, count, chunk), BF16),
            vmem((rows, count), F32),
            vmem((m, rows, count), F32),
            vmem((count, count), F32),
            vmem((count, cols), BF16),
            vmem((n, 8, 128), F32),
            dma(()), dma(()), dma((1,)), dma((chunks,)),
            dma((2, lines)), dma((lines, per_line)), dma((lines, per_line)),
            dma((n,)),
            dma((m,)), dma((m,)), dma((n,)), dma((n,)), dma((m,)), dma((m,)),
            dma((2, chunks, m)), dma((2, m, chunks)),
            dma((m,)), dma((m,)), dma((n,)), dma((n,)), dma((n,)), dma((n,)),
        ],
        compiler_params=pltpu.CompilerParams(
            collective_id=0, has_side_effects=True, vmem_limit_bytes=56 * 2**20
        ),
        name="slopes",
    )(tokens, norm_gain.reshape(1, depth), w_up, cotangent)

    return pl.pallas_call(
        grad_kernel,
        grid=(depth // 256,),
        out_shape=jax.ShapeDtypeStruct((depth, cols), F32),
        in_specs=[
            pl.BlockSpec((256, count), lambda i: (i, 0)),
            pl.BlockSpec((count, cols), lambda i: (0, 0)),
        ],
        out_specs=pl.BlockSpec((256, cols), lambda i: (i, 0)),
        compiler_params=pltpu.CompilerParams(vmem_limit_bytes=60 * 2**20),
        name="grad",
    )(nt, slope)


def solution(mesh):
    placed = (P("dp", "mp"), P("mp"), P("mp", "dp"), P("mp", "dp"))
    return jax.shard_map(
        per_device, mesh=mesh, in_specs=placed, out_specs=P("mp", "dp"), check_vma=False
    )
```

```python
import functools
import math

import jax
import jax.numpy as jnp
from jax import lax
from jax.experimental import pallas as pl
from jax.experimental.pallas import tpu as pltpu
from jax.sharding import PartitionSpec as P

FF = 24576
MESH = pl.DeviceIdType.MESH
F32 = jnp.float32
BF16 = jnp.bfloat16


def gelu_slope(value):
    cdf = 0.5 * (1.0 + lax.erf(value * (1.0 / math.sqrt(2.0))))
    dens = jnp.exp(-0.5 * value * value) * (1.0 / math.sqrt(2.0 * math.pi))
    return cdf + value * dens


def remote(src, dst, send_sem, recv_sem, device):
    return pltpu.make_async_remote_copy(
        src_ref=src, dst_ref=dst, send_sem=send_sem, recv_sem=recv_sem,
        device_id=device, device_id_type=MESH,
    )


def slopes_kernel(
    cfg,
    tok_ref, gain_ref, w_hbm, cot_hbm,
    nt_hbm, slope_hbm,
    nt_ref, pre_ref, gs_ref, cot_ref, g_terms, nlocal,
    xs, nall, w, st_part, st_part_in, st_all, own, sendb, recvb,
    g_part, g_part_in, g_all, slope, nb,
    w_sem, c_sem, o_sem, slope_os, z_ss, y_ss, core_ss, x_rs,
    stp_ss, stp_rs, st_ss, st_rs, cot_ss, cot_rs, pre_ss, pre_rs,
    gp_ss, gp_rs, g_ss, g_rs, nb_ss, nb_rs,
):
    n, m, lines, width_all, token_count = cfg
    rows, depth = tok_ref.shape
    cot_rows, cols = cot_hbm.shape
    chunks, _, chunk = own.shape
    cores = 2
    per_line = n // (lines * cores)
    scale = 1.0 / math.sqrt(token_count)
    me = lax.axis_index("dp")
    my_mp = lax.axis_index("mp")
    core = lax.rem(me, cores)
    across = lax.rem(me // cores, per_line)
    along = me // (cores * per_line)

    group = rows * cores
    near = lines * group
    parts = [(0, near), (near, token_count - near)]

    def index(a, b, c):
        return (a * per_line + b) * cores + c

    def dp_peer(k):
        return lax.rem(me + k, n)

    def mp_peer(k):
        return lax.rem(my_mp + k, m)

    w_copy = pltpu.make_async_copy(w_hbm, w, w_sem)
    w_copy.start()
    cot_dst = cot_ref.at[pl.ds(pl.multiple_of(my_mp * cot_rows, cot_rows), cot_rows)]
    cot_copy = pltpu.make_async_copy(cot_hbm, cot_dst, c_sem)
    cot_copy.start()

    barrier = pltpu.get_barrier_semaphore()

    @pl.loop(1, n)
    def _(k):
        pl.semaphore_signal(barrier, inc=1, device_id={"dp": dp_peer(k)}, device_id_type=MESH)

    @pl.loop(1, m)
    def _(k):
        pl.semaphore_signal(barrier, inc=1, device_id={"mp": mp_peer(k)}, device_id_type=MESH)

    values = tok_ref[...].astype(F32)
    lane = lax.broadcasted_iota(jnp.int32, (rows, 128), 1)
    sums = jnp.sum(values, axis=1, keepdims=True)
    squares = jnp.sum(values * values, axis=1, keepdims=True)
    st_part[...] = jnp.where(lane == 0, sums, squares)
    xs[me] = tok_ref[...]

    pl.semaphore_wait(barrier, n + m - 2)

    def line_copy(src_a, up):
        src = index(src_a, across, core)
        to = index(along + 1 if up else along - 1, across, core)
        return remote(xs.at[src], xs.at[src], z_ss.at[int(up), src_a], x_rs.at[src], {"dp": to})

    def across_copy(src_a, j):
        src = index(src_a, across, core)
        to = index(along, lax.rem(across + j, per_line), core)
        return remote(xs.at[src], xs.at[src], y_ss.at[src_a, j], x_rs.at[src], {"dp": to})

    def core_copy(src_a, j):
        src = index(src_a, lax.rem(across + j, per_line), core)
        return remote(xs.at[src], xs.at[src], core_ss.at[src_a, j], x_rs.at[src],
                      {"dp": index(along, across, 1 - core)})

    def arrived(src):
        remote(xs.at[src], xs.at[src], z_ss.at[0, 0], x_rs.at[src], {"dp": dp_peer(1)}).wait_recv()

    by_distance = [(along - s if low else along + s, low) for s in range(1, lines) for low in (True, False)]

    def there(pos, low):
        return pos >= 0 if low else pos < lines

    def can_go(up):
        return along + 1 < lines if up else along > 0

    def across_step(pos):
        for j in range(1, per_line):
            arrived(index(pos, lax.rem(across + j, per_line), core))
            core_copy(pos, j).start()

    def stp_copy(k):
        return remote(st_part, st_part_in.at[my_mp], stp_ss.at[k], stp_rs.at[my_mp],
                      {"mp": mp_peer(k)})

    def cot_send(k):
        return remote(cot_hbm, cot_dst, cot_ss.at[k], cot_rs.at[my_mp], {"mp": mp_peer(k)})

    for k in range(1, m):
        stp_copy(k).start()
    for k in range(1, m):
        cot_send(k).start()
    for up in (True, False):
        @pl.when(can_go(up))
        def _():
            line_copy(along, up).start()
    for j in range(1, per_line):
        across_copy(along, j).start()
    core_copy(along, 0).start()

    total = st_part[...]
    for k in range(1, m):
        p = mp_peer(k)
        remote(st_part, st_part_in.at[p], stp_ss.at[0], stp_rs.at[p], {"mp": p}).wait_recv()
        total = total + st_part_in[p]
    mean = total[:, 0:1] / width_all
    var = total[:, 1:2] / width_all - mean * mean
    st_all[me] = jnp.where(lane == 0, mean, lax.rsqrt(var + 1e-06))

    def st_copy(k):
        return remote(st_all.at[me], st_all.at[me], st_ss.at[k], st_rs.at[me],
                      {"dp": dp_peer(k)})

    @pl.loop(1, n)
    def _(k):
        st_copy(k).start()

    for pos, low in by_distance:
        @pl.when(there(pos, low))
        def _():
            arrived(index(pos, across, core))

            @pl.when(can_go(low))
            def _():
                line_copy(pos, low).start()

            for j in range(1, per_line):
                across_copy(pos, j).start()
            core_copy(pos, 0).start()

    @pl.loop(1, n)
    def _(k):
        p = dp_peer(k)
        remote(st_all.at[p], st_all.at[p], st_ss.at[0], st_rs.at[p], {"dp": p}).wait_recv()

    def normalize(src):
        x = xs[src].astype(F32)
        st = st_all[src]
        value = ((x - st[:, 0:1]) * st[:, 1:2] * gain_ref[...]).astype(BF16)
        nall[pl.ds(pl.multiple_of(src * rows, rows), rows), :] = value
        a = src // (cores * per_line)
        p = lax.rem(lax.rem(src // cores, per_line) + per_line - across, per_line)
        local = ((p * lines + a) * cores + lax.rem(src, cores)) * rows
        nlocal[pl.ds(pl.multiple_of(local, rows), rows), :] = value

    @pl.loop(0, lines)
    def _(k):
        normalize(index(lax.rem(along + k, lines), across, core))

    @pl.loop(0, lines)
    def _(k):
        src = index(lax.rem(along + k, lines), across, 1 - core)
        arrived(src)
        normalize(src)

    w_copy.wait()

    def pre_copy(part, i, k):
        at, size = parts[part]
        return remote(sendb.at[i, pl.ds(at, size)], recvb.at[my_mp, i, pl.ds(at, size)],
                      pre_ss.at[part, i, k], pre_rs.at[part, my_mp, i], {"mp": mp_peer(k)})

    def project(part, i):
        at, size = parts[part]
        off = pl.multiple_of(i * chunk, chunk)
        value = jnp.dot(nlocal[pl.ds(at, size), :], w[:, pl.ds(off, chunk)],
                        preferred_element_type=F32)
        own[i, pl.ds(at, size)] = value
        sendb[i, pl.ds(at, size)] = value.astype(BF16)
        for k in range(1, m):
            pre_copy(part, i, k).start()

    first = 1

    @pl.loop(0, first)
    def _(i):
        project(0, i)

    across_step(along)
    for pos, low in by_distance:
        @pl.when(there(pos, low))
        def _():
            across_step(pos)

    @pl.loop(first, chunks)
    def _(i):
        project(0, i)

    @pl.loop(0, lines * (per_line - 1))
    def _(i):
        k = i // (per_line - 1)
        j = 1 + lax.rem(i, per_line - 1)
        normalize(index(lax.rem(along + k, lines), lax.rem(across + j, per_line), core))

    @pl.loop(0, lines * (per_line - 1))
    def _(i):
        k = i // (per_line - 1)
        j = 1 + lax.rem(i, per_line - 1)
        src = index(lax.rem(along + k, lines), lax.rem(across + j, per_line), 1 - core)
        arrived(src)
        normalize(src)

    mine = pl.ds(pl.multiple_of(me * rows, rows), rows)
    g_part[...] = lax.dot_general(
        nall[mine, :], nall[...], (((1,), (1,)), ((), ())), preferred_element_type=F32
    )

    def gp_copy(k):
        return remote(g_part, g_part_in.at[my_mp], gp_ss.at[k], gp_rs.at[my_mp],
                      {"mp": mp_peer(k)})

    def g_copy(k):
        return remote(g_all.at[mine], g_all.at[mine], g_ss.at[k], g_rs.at[me],
                      {"dp": dp_peer(k)})

    for k in range(1, m):
        gp_copy(k).start()

    @pl.loop(0, chunks)
    def _(i):
        project(1, i)

    @pl.loop(0, depth // 256)
    def _(i):
        off = pl.multiple_of(i * 256, 256)
        nt_ref[pl.ds(off, 256), :] = nall[:, pl.ds(off, 256)].T

    nt_copy = pltpu.make_async_copy(nt_ref, nt_hbm, o_sem.at[0])
    nt_copy.start()

    cot_copy.wait()
    for k in range(1, m):
        p = mp_peer(k)
        dst = cot_ref.at[pl.ds(pl.multiple_of(p * cot_rows, cot_rows), cot_rows)]
        remote(cot_hbm, dst, cot_ss.at[0], cot_rs.at[p], {"mp": p}).wait_recv()

    def local_groups(part):
        at, size = parts[part]
        for g in range(at // group, (at + size) // group):
            p, a = g // lines, g % lines
            row = (a * per_line + lax.rem(across + p, per_line)) * group
            yield pl.ds(pl.multiple_of(row, group), group)

    def first_slopes(part, i):
        at, size = parts[part]
        off = pl.multiple_of(i * chunk, chunk)
        pre = own[i, pl.ds(at, size)]
        for k in range(1, m):
            p = mp_peer(k)
            remote(sendb.at[i, pl.ds(at, size)], recvb.at[p, i, pl.ds(at, size)],
                   pre_ss.at[part, i, 0], pre_rs.at[part, p, i], {"mp": p}).wait_recv()
            pre = pre + recvb[p, i, pl.ds(at, size)].astype(F32)
        cot = jnp.concatenate([cot_ref[r, pl.ds(off, chunk)] for r in local_groups(part)], axis=0)
        s = (cot.astype(F32) * gelu_slope(pre) * scale).astype(BF16)
        for g, r in enumerate(local_groups(part)):
            pre_ref[r, pl.ds(off, chunk)] = pre[g * group:(g + 1) * group]
            slope[r, pl.ds(off, chunk)] = s[g * group:(g + 1) * group]

    @pl.loop(0, chunks)
    def _(i):
        first_slopes(0, i)

    gram = g_part[...]
    for k in range(1, m):
        p = mp_peer(k)
        remote(g_part, g_part_in.at[p], gp_ss.at[0], gp_rs.at[p], {"mp": p}).wait_recv()
        gram = gram + g_part_in[p]
    g_all[mine, :] = gram

    @pl.loop(1, n)
    def _(k):
        g_copy(k).start()

    @pl.loop(1, n)
    def _(k):
        p = dp_peer(k)
        dst = g_all.at[pl.ds(pl.multiple_of(p * rows, rows), rows)]
        remote(dst, dst, g_ss.at[0], g_rs.at[p], {"dp": p}).wait_recv()

    rest = g_all[...]
    for t in range(3):
        g_terms[t] = rest.astype(BF16)
        rest = rest - g_terms[t].astype(F32)

    nb[me] = jnp.zeros_like(nb[me])

    @pl.loop(0, chunks)
    def _(i):
        first_slopes(1, i)
        off = pl.multiple_of(i * chunk, chunk)
        s = slope[:, pl.ds(off, chunk)]
        gs = (
            jnp.dot(g_terms[2], s, preferred_element_type=F32)
            + jnp.dot(g_terms[1], s, preferred_element_type=F32)
            + jnp.dot(g_terms[0], s, preferred_element_type=F32)
        )
        gs_ref[:, pl.ds(off, chunk)] = gs
        nb[me] += jnp.full((8, 128), jnp.sum(gs * s.astype(F32)), F32)

    def nb_copy(k):
        return remote(nb.at[me], nb.at[me], nb_ss.at[k], nb_rs.at[me], {"dp": dp_peer(k)})

    @pl.loop(1, n)
    def _(k):
        nb_copy(k).start()

    @pl.loop(1, n)
    def _(k):
        st_copy(k).wait_send()
        g_copy(k).wait_send()

    for pos, low in [(along, True), (along, False)] + by_distance:
        @pl.when(jnp.logical_and(there(pos, low), can_go(low)))
        def _():
            line_copy(pos, low).wait_send()

    @pl.loop(0, lines)
    def _(pos):
        for j in range(per_line):
            core_copy(pos, j).wait_send()
            if j > 0:
                across_copy(pos, j).wait_send()

    for k in range(1, m):
        stp_copy(k).wait_send()
        cot_send(k).wait_send()
        gp_copy(k).wait_send()

        @pl.loop(0, chunks)
        def _(i):
            pre_copy(0, i, k).wait_send()
            pre_copy(1, i, k).wait_send()

    @pl.loop(1, n)
    def _(k):
        p = dp_peer(k)
        remote(nb.at[p], nb.at[p], nb_ss.at[0], nb_rs.at[p], {"dp": p}).wait_recv()
        nb_copy(k).wait_send()

    squared = jnp.sum(nb[...], axis=0)[0:1, 0:1]
    size = jnp.sqrt(jnp.maximum(squared, 0.0)) + 1e-12
    radius = 0.5 * math.sqrt(FF)

    def slope_copy(i):
        at = pl.ds(pl.multiple_of(i * chunk, chunk), chunk)
        return pltpu.make_async_copy(slope.at[:, at], slope_hbm.at[:, at], slope_os.at[i])

    @pl.loop(0, chunks)
    def _(i):
        at = pl.ds(pl.multiple_of(i * chunk, chunk), chunk)
        pre = pre_ref[:, at] + radius * gs_ref[:, at] / size
        slope[:, at] = (cot_ref[:, at].astype(F32) * gelu_slope(pre) * scale).astype(BF16)
        slope_copy(i).start()

    nt_copy.wait()

    @pl.loop(0, chunks)
    def _(i):
        slope_copy(i).wait()


def grad_kernel(nt_ref, slope_ref, out_ref):
    out_ref[...] = jnp.dot(nt_ref[...], slope_ref[...], preferred_element_type=F32)


def per_device(tokens, norm_gain, w_up, cotangent):
    n, m = lax.axis_size("dp"), lax.axis_size("mp")
    rows, depth = tokens.shape
    count = rows * n
    cols = w_up.shape[1]
    lines = 4
    chunk = next(c for c in (512, 256, 128) if cols % c == 0)
    narrow = min(chunk, 256)
    chunks = cols // chunk
    per_line = n // (2 * lines)
    cot_rows = cotangent.shape[0]
    dma, vmem = pltpu.SemaphoreType.DMA, pltpu.VMEM
    whole = pl.BlockSpec(memory_space=pltpu.VMEM)
    hbm = pl.BlockSpec(memory_space=pl.ANY)
    cfg = (n, m, lines, depth * m, count)
    nt, slope = pl.pallas_call(
        functools.partial(slopes_kernel, cfg),
        out_shape=(
            jax.ShapeDtypeStruct((depth, count), BF16),
            jax.ShapeDtypeStruct((count, cols), BF16),
        ),
        in_specs=[whole, whole, hbm, hbm],
        out_specs=[hbm] * 2,
        scratch_shapes=[
            vmem((depth, count), BF16),
            vmem((count, cols), F32),
            vmem((count, cols), F32),
            vmem((count, cols), BF16),
            vmem((3, count, count), BF16),
            vmem((count, depth), BF16),
            vmem((n, rows, depth), BF16),
            vmem((count, depth), BF16),
            vmem((depth, cols), BF16),
            vmem((rows, 128), F32),
            vmem((m, rows, 128), F32),
            vmem((n, rows, 128), F32),
            vmem((chunks, count, chunk), F32),
            vmem((chunks, count, chunk), BF16),
            vmem((m, chunks, count, chunk), BF16),
            vmem((rows, count), F32),
            vmem((m, rows, count), F32),
            vmem((count, count), F32),
            vmem((count, cols), BF16),
            vmem((n, 8, 128), F32),
            dma(()), dma(()), dma((1,)), dma((chunks,)),
            dma((2, lines)), dma((lines, per_line)), dma((lines, per_line)),
            dma((n,)),
            dma((m,)), dma((m,)), dma((n,)), dma((n,)), dma((m,)), dma((m,)),
            dma((2, chunks, m)), dma((2, m, chunks)),
            dma((m,)), dma((m,)), dma((n,)), dma((n,)), dma((n,)), dma((n,)),
        ],
        compiler_params=pltpu.CompilerParams(
            collective_id=0, has_side_effects=True, vmem_limit_bytes=56 * 2**20
        ),
        name="slopes",
    )(tokens, norm_gain.reshape(1, depth), w_up, cotangent)

    return pl.pallas_call(
        grad_kernel,
        grid=(2, cols // narrow),
        out_shape=jax.ShapeDtypeStruct((depth, cols), F32),
        in_specs=[
            pl.BlockSpec((depth // 2, count), lambda i, j: (i, 0)),
            pl.BlockSpec((count, narrow), lambda i, j: (0, j)),
        ],
        out_specs=pl.BlockSpec((depth // 2, narrow), lambda i, j: (i, j)),
        compiler_params=pltpu.CompilerParams(vmem_limit_bytes=60 * 2**20),
        name="grad",
    )(nt, slope)


def solution(mesh):
    placed = (P("dp", "mp"), P("mp"), P("mp", "dp"), P("mp", "dp"))
    return jax.shard_map(
        per_device, mesh=mesh, in_specs=placed, out_specs=P("mp", "dp"), check_vma=False
    )
```

```python
import functools
import math

import jax
import jax.numpy as jnp
from jax import lax
from jax.experimental import pallas as pl
from jax.experimental.pallas import tpu as pltpu
from jax.sharding import PartitionSpec as P

FF = 24576
MESH = pl.DeviceIdType.MESH
F32 = jnp.float32
BF16 = jnp.bfloat16


def gelu_slope(value):
    cdf = 0.5 * (1.0 + lax.erf(value * (1.0 / math.sqrt(2.0))))
    dens = jnp.exp(-0.5 * value * value) * (1.0 / math.sqrt(2.0 * math.pi))
    return cdf + value * dens


def remote(src, dst, send_sem, recv_sem, device):
    return pltpu.make_async_remote_copy(
        src_ref=src, dst_ref=dst, send_sem=send_sem, recv_sem=recv_sem,
        device_id=device, device_id_type=MESH,
    )


def slopes_kernel(
    cfg,
    tok_ref, gain_ref, w_hbm, cot_hbm,
    nt_hbm, slope_hbm,
    nt_ref, pre_ref, gs_ref, cot_ref, g_terms, nlocal,
    xs, nall, w, st_part, st_part_in, st_all, own, sendb, recvb,
    g_part, g_part_in, g_all, slope, nb,
    w_sem, c_sem, o_sem, slope_os, z_ss, y_ss, core_ss, x_rs,
    stp_ss, stp_rs, st_ss, st_rs, cot_ss, cot_rs, pre_ss, pre_rs,
    gp_ss, gp_rs, g_ss, g_rs, nb_ss, nb_rs,
):
    n, m, lines, width_all, token_count = cfg
    rows, depth = tok_ref.shape
    cot_rows, cols = cot_hbm.shape
    chunks, _, chunk = own.shape
    cores = 2
    per_line = n // (lines * cores)
    scale = 1.0 / math.sqrt(token_count)
    me = lax.axis_index("dp")
    my_mp = lax.axis_index("mp")
    core = lax.rem(me, cores)
    across = lax.rem(me // cores, per_line)
    along = me // (cores * per_line)

    group = rows * cores
    near = lines * group
    parts = [(0, near), (near, token_count - near)]

    def index(a, b, c):
        return (a * per_line + b) * cores + c

    def dp_peer(k):
        return lax.rem(me + k, n)

    def mp_peer(k):
        return lax.rem(my_mp + k, m)

    w_copy = pltpu.make_async_copy(w_hbm, w, w_sem)
    w_copy.start()
    cot_dst = cot_ref.at[pl.ds(pl.multiple_of(my_mp * cot_rows, cot_rows), cot_rows)]
    cot_copy = pltpu.make_async_copy(cot_hbm, cot_dst, c_sem)
    cot_copy.start()

    barrier = pltpu.get_barrier_semaphore()

    @pl.loop(1, n)
    def _(k):
        pl.semaphore_signal(barrier, inc=1, device_id={"dp": dp_peer(k)}, device_id_type=MESH)

    @pl.loop(1, m)
    def _(k):
        pl.semaphore_signal(barrier, inc=1, device_id={"mp": mp_peer(k)}, device_id_type=MESH)

    values = tok_ref[...].astype(F32)
    lane = lax.broadcasted_iota(jnp.int32, (rows, 128), 1)
    sums = jnp.sum(values, axis=1, keepdims=True)
    squares = jnp.sum(values * values, axis=1, keepdims=True)
    st_part[...] = jnp.where(lane == 0, sums, squares)
    xs[me] = tok_ref[...]

    pl.semaphore_wait(barrier, n + m - 2)

    def line_copy(src_a, up):
        src = index(src_a, across, core)
        to = index(along + 1 if up else along - 1, across, core)
        return remote(xs.at[src], xs.at[src], z_ss.at[int(up), src_a], x_rs.at[src], {"dp": to})

    def across_copy(src_a, j):
        src = index(src_a, across, core)
        to = index(along, lax.rem(across + j, per_line), core)
        return remote(xs.at[src], xs.at[src], y_ss.at[src_a, j], x_rs.at[src], {"dp": to})

    def core_copy(src_a, j):
        src = index(src_a, lax.rem(across + j, per_line), core)
        return remote(xs.at[src], xs.at[src], core_ss.at[src_a, j], x_rs.at[src],
                      {"dp": index(along, across, 1 - core)})

    def arrived(src):
        remote(xs.at[src], xs.at[src], z_ss.at[0, 0], x_rs.at[src], {"dp": dp_peer(1)}).wait_recv()

    by_distance = [(along - s if low else along + s, low) for s in range(1, lines) for low in (True, False)]

    def there(pos, low):
        return pos >= 0 if low else pos < lines

    def can_go(up):
        return along + 1 < lines if up else along > 0

    def across_step(pos):
        for j in range(1, per_line):
            arrived(index(pos, lax.rem(across + j, per_line), core))
            core_copy(pos, j).start()

    def stp_copy(k):
        return remote(st_part, st_part_in.at[my_mp], stp_ss.at[k], stp_rs.at[my_mp],
                      {"mp": mp_peer(k)})

    def cot_send(k):
        return remote(cot_hbm, cot_dst, cot_ss.at[k], cot_rs.at[my_mp], {"mp": mp_peer(k)})

    for k in range(1, m):
        stp_copy(k).start()
    for k in range(1, m):
        cot_send(k).start()
    for up in (True, False):
        @pl.when(can_go(up))
        def _():
            line_copy(along, up).start()
    for j in range(1, per_line):
        across_copy(along, j).start()
    core_copy(along, 0).start()

    def relay(pos, low):
        @pl.when(there(pos, low))
        def _():
            arrived(index(pos, across, core))

            @pl.when(can_go(low))
            def _():
                line_copy(pos, low).start()

            for j in range(1, per_line):
                across_copy(pos, j).start()
            core_copy(pos, 0).start()

    for pos, low in by_distance[:2]:
        relay(pos, low)

    total = st_part[...]
    for k in range(1, m):
        p = mp_peer(k)
        remote(st_part, st_part_in.at[p], stp_ss.at[0], stp_rs.at[p], {"mp": p}).wait_recv()
        total = total + st_part_in[p]
    mean = total[:, 0:1] / width_all
    var = total[:, 1:2] / width_all - mean * mean
    st_all[me] = jnp.where(lane == 0, mean, lax.rsqrt(var + 1e-06))

    def st_copy(k):
        return remote(st_all.at[me], st_all.at[me], st_ss.at[k], st_rs.at[me],
                      {"dp": dp_peer(k)})

    @pl.loop(1, n)
    def _(k):
        st_copy(k).start()

    for pos, low in by_distance[2:]:
        relay(pos, low)

    @pl.loop(1, n)
    def _(k):
        p = dp_peer(k)
        remote(st_all.at[p], st_all.at[p], st_ss.at[0], st_rs.at[p], {"dp": p}).wait_recv()

    def normalize(src):
        x = xs[src].astype(F32)
        st = st_all[src]
        value = ((x - st[:, 0:1]) * st[:, 1:2] * gain_ref[...]).astype(BF16)
        nall[pl.ds(pl.multiple_of(src * rows, rows), rows), :] = value
        a = src // (cores * per_line)
        p = lax.rem(lax.rem(src // cores, per_line) + per_line - across, per_line)
        local = ((p * lines + a) * cores + lax.rem(src, cores)) * rows
        nlocal[pl.ds(pl.multiple_of(local, rows), rows), :] = value

    @pl.loop(0, lines)
    def _(k):
        normalize(index(lax.rem(along + k, lines), across, core))

    @pl.loop(0, lines)
    def _(k):
        src = index(lax.rem(along + k, lines), across, 1 - core)
        arrived(src)
        normalize(src)

    w_copy.wait()

    def pre_copy(part, i, k):
        at, size = parts[part]
        return remote(sendb.at[i, pl.ds(at, size)], recvb.at[my_mp, i, pl.ds(at, size)],
                      pre_ss.at[part, i, k], pre_rs.at[part, my_mp, i], {"mp": mp_peer(k)})

    def project(part, i):
        at, size = parts[part]
        off = pl.multiple_of(i * chunk, chunk)
        value = jnp.dot(nlocal[pl.ds(at, size), :], w[:, pl.ds(off, chunk)],
                        preferred_element_type=F32)
        own[i, pl.ds(at, size)] = value
        sendb[i, pl.ds(at, size)] = value.astype(BF16)
        for k in range(1, m):
            pre_copy(part, i, k).start()

    first = 1

    @pl.loop(0, first)
    def _(i):
        project(0, i)

    across_step(along)
    for pos, low in by_distance:
        @pl.when(there(pos, low))
        def _():
            across_step(pos)

    @pl.loop(first, chunks)
    def _(i):
        project(0, i)

    @pl.loop(0, lines * (per_line - 1))
    def _(i):
        k = i // (per_line - 1)
        j = 1 + lax.rem(i, per_line - 1)
        normalize(index(lax.rem(along + k, lines), lax.rem(across + j, per_line), core))

    @pl.loop(0, lines * (per_line - 1))
    def _(i):
        k = i // (per_line - 1)
        j = 1 + lax.rem(i, per_line - 1)
        src = index(lax.rem(along + k, lines), lax.rem(across + j, per_line), 1 - core)
        arrived(src)
        normalize(src)

    mine = pl.ds(pl.multiple_of(me * rows, rows), rows)
    g_part[...] = lax.dot_general(
        nall[mine, :], nall[...], (((1,), (1,)), ((), ())), preferred_element_type=F32
    )

    def gp_copy(k):
        return remote(g_part, g_part_in.at[my_mp], gp_ss.at[k], gp_rs.at[my_mp],
                      {"mp": mp_peer(k)})

    def g_copy(k):
        return remote(g_all.at[mine], g_all.at[mine], g_ss.at[k], g_rs.at[me],
                      {"dp": dp_peer(k)})

    for k in range(1, m):
        gp_copy(k).start()

    @pl.loop(0, chunks)
    def _(i):
        project(1, i)

    gram = g_part[...]
    for k in range(1, m):
        p = mp_peer(k)
        remote(g_part, g_part_in.at[p], gp_ss.at[0], gp_rs.at[p], {"mp": p}).wait_recv()
        gram = gram + g_part_in[p]
    g_all[mine, :] = gram

    @pl.loop(1, n)
    def _(k):
        g_copy(k).start()

    cot_copy.wait()
    for k in range(1, m):
        p = mp_peer(k)
        dst = cot_ref.at[pl.ds(pl.multiple_of(p * cot_rows, cot_rows), cot_rows)]
        remote(cot_hbm, dst, cot_ss.at[0], cot_rs.at[p], {"mp": p}).wait_recv()

    def local_groups(part):
        at, size = parts[part]
        for g in range(at // group, (at + size) // group):
            p, a = g // lines, g % lines
            row = (a * per_line + lax.rem(across + p, per_line)) * group
            yield pl.ds(pl.multiple_of(row, group), group)

    def first_slopes(part, i):
        at, size = parts[part]
        off = pl.multiple_of(i * chunk, chunk)
        pre = own[i, pl.ds(at, size)]
        for k in range(1, m):
            p = mp_peer(k)
            remote(sendb.at[i, pl.ds(at, size)], recvb.at[p, i, pl.ds(at, size)],
                   pre_ss.at[part, i, 0], pre_rs.at[part, p, i], {"mp": p}).wait_recv()
            pre = pre + recvb[p, i, pl.ds(at, size)].astype(F32)
        cot = jnp.concatenate([cot_ref[r, pl.ds(off, chunk)] for r in local_groups(part)], axis=0)
        s = (cot.astype(F32) * gelu_slope(pre) * scale).astype(BF16)
        for g, r in enumerate(local_groups(part)):
            pre_ref[r, pl.ds(off, chunk)] = pre[g * group:(g + 1) * group]
            slope[r, pl.ds(off, chunk)] = s[g * group:(g + 1) * group]

    @pl.loop(0, chunks)
    def _(i):
        first_slopes(0, i)

    @pl.loop(1, n)
    def _(k):
        p = dp_peer(k)
        dst = g_all.at[pl.ds(pl.multiple_of(p * rows, rows), rows)]
        remote(dst, dst, g_ss.at[0], g_rs.at[p], {"dp": p}).wait_recv()

    rest = g_all[...]
    for t in range(3):
        term = rest.astype(BF16)
        g_terms[t * token_count:(t + 1) * token_count] = term
        rest = rest - term.astype(F32)

    nb[me] = jnp.zeros_like(nb[me])

    @pl.loop(0, chunks)
    def _(i):
        first_slopes(1, i)
        off = pl.multiple_of(i * chunk, chunk)
        s = slope[:, pl.ds(off, chunk)]
        terms = jnp.dot(g_terms[...], s, preferred_element_type=F32)
        t = token_count
        gs = terms[2 * t:] + terms[t:2 * t] + terms[:t]
        gs_ref[:, pl.ds(off, chunk)] = gs
        nb[me] += jnp.full((8, 128), jnp.sum(gs * s.astype(F32)), F32)

    def nb_copy(k):
        return remote(nb.at[me], nb.at[me], nb_ss.at[k], nb_rs.at[me], {"dp": dp_peer(k)})

    @pl.loop(1, n)
    def _(k):
        nb_copy(k).start()

    @pl.loop(0, depth // 256)
    def _(i):
        off = pl.multiple_of(i * 256, 256)
        nt_ref[pl.ds(off, 256), :] = nall[:, pl.ds(off, 256)].T

    nt_copy = pltpu.make_async_copy(nt_ref, nt_hbm, o_sem.at[0])
    nt_copy.start()

    @pl.loop(1, n)
    def _(k):
        st_copy(k).wait_send()
        g_copy(k).wait_send()

    for pos, low in [(along, True), (along, False)] + by_distance:
        @pl.when(jnp.logical_and(there(pos, low), can_go(low)))
        def _():
            line_copy(pos, low).wait_send()

    @pl.loop(0, lines)
    def _(pos):
        for j in range(per_line):
            core_copy(pos, j).wait_send()
            if j > 0:
                across_copy(pos, j).wait_send()

    for k in range(1, m):
        stp_copy(k).wait_send()
        cot_send(k).wait_send()
        gp_copy(k).wait_send()

        @pl.loop(0, chunks)
        def _(i):
            pre_copy(0, i, k).wait_send()
            pre_copy(1, i, k).wait_send()

    @pl.loop(1, n)
    def _(k):
        p = dp_peer(k)
        remote(nb.at[p], nb.at[p], nb_ss.at[0], nb_rs.at[p], {"dp": p}).wait_recv()
        nb_copy(k).wait_send()

    squared = jnp.sum(nb[...], axis=0)[0:1, 0:1]
    size = jnp.sqrt(jnp.maximum(squared, 0.0)) + 1e-12
    radius = 0.5 * math.sqrt(FF)

    def slope_copy(i):
        at = pl.ds(pl.multiple_of(i * chunk, chunk), chunk)
        return pltpu.make_async_copy(slope.at[:, at], slope_hbm.at[:, at], slope_os.at[i])

    @pl.loop(0, chunks)
    def _(i):
        at = pl.ds(pl.multiple_of(i * chunk, chunk), chunk)
        pre = pre_ref[:, at] + radius * gs_ref[:, at] / size
        slope[:, at] = (cot_ref[:, at].astype(F32) * gelu_slope(pre) * scale).astype(BF16)
        slope_copy(i).start()

    nt_copy.wait()

    @pl.loop(0, chunks)
    def _(i):
        slope_copy(i).wait()


def grad_kernel(nt_hbm, slope_hbm, out_hbm, nt, slope, out, nt_sem, slope_sem, out_sem):
    blocks = nt_sem.shape[0]
    rows = nt.shape[0] // blocks

    def cut(i):
        return pl.ds(pl.multiple_of(i * rows, rows), rows)

    def nt_copy(i):
        return pltpu.make_async_copy(nt_hbm.at[cut(i)], nt.at[cut(i)], nt_sem.at[i])

    def out_copy(i):
        return pltpu.make_async_copy(out.at[cut(i)], out_hbm.at[cut(i)], out_sem.at[i])

    slope_copy = pltpu.make_async_copy(slope_hbm, slope, slope_sem)
    slope_copy.start()

    @pl.loop(0, blocks)
    def _(i):
        nt_copy(i).start()

    slope_copy.wait()

    @pl.loop(0, blocks)
    def _(i):
        nt_copy(i).wait()
        out[cut(i), :] = jnp.dot(nt[cut(i), :], slope[...], preferred_element_type=F32)
        out_copy(i).start()

    @pl.loop(0, blocks)
    def _(i):
        out_copy(i).wait()


def per_device(tokens, norm_gain, w_up, cotangent):
    n, m = lax.axis_size("dp"), lax.axis_size("mp")
    rows, depth = tokens.shape
    count = rows * n
    cols = w_up.shape[1]
    lines = 4
    chunk = next(c for c in (512, 256, 128) if cols % c == 0)
    chunks = cols // chunk
    per_line = n // (2 * lines)
    cot_rows = cotangent.shape[0]
    dma, vmem = pltpu.SemaphoreType.DMA, pltpu.VMEM
    whole = pl.BlockSpec(memory_space=pltpu.VMEM)
    hbm = pl.BlockSpec(memory_space=pl.ANY)
    cfg = (n, m, lines, depth * m, count)
    nt, slope = pl.pallas_call(
        functools.partial(slopes_kernel, cfg),
        out_shape=(
            jax.ShapeDtypeStruct((depth, count), BF16),
            jax.ShapeDtypeStruct((count, cols), BF16),
        ),
        in_specs=[whole, whole, hbm, hbm],
        out_specs=[hbm] * 2,
        scratch_shapes=[
            vmem((depth, count), BF16),
            vmem((count, cols), F32),
            vmem((count, cols), F32),
            vmem((count, cols), BF16),
            vmem((3 * count, count), BF16),
            vmem((count, depth), BF16),
            vmem((n, rows, depth), BF16),
            vmem((count, depth), BF16),
            vmem((depth, cols), BF16),
            vmem((rows, 128), F32),
            vmem((m, rows, 128), F32),
            vmem((n, rows, 128), F32),
            vmem((chunks, count, chunk), F32),
            vmem((chunks, count, chunk), BF16),
            vmem((m, chunks, count, chunk), BF16),
            vmem((rows, count), F32),
            vmem((m, rows, count), F32),
            vmem((count, count), F32),
            vmem((count, cols), BF16),
            vmem((n, 8, 128), F32),
            dma(()), dma(()), dma((1,)), dma((chunks,)),
            dma((2, lines)), dma((lines, per_line)), dma((lines, per_line)),
            dma((n,)),
            dma((m,)), dma((m,)), dma((n,)), dma((n,)), dma((m,)), dma((m,)),
            dma((2, chunks, m)), dma((2, m, chunks)),
            dma((m,)), dma((m,)), dma((n,)), dma((n,)), dma((n,)), dma((n,)),
        ],
        compiler_params=pltpu.CompilerParams(
            collective_id=0, has_side_effects=True, vmem_limit_bytes=56 * 2**20
        ),
        name="slopes",
    )(tokens, norm_gain.reshape(1, depth), w_up, cotangent)

    return pl.pallas_call(
        grad_kernel,
        out_shape=jax.ShapeDtypeStruct((depth, cols), F32),
        in_specs=[hbm, hbm],
        out_specs=hbm,
        scratch_shapes=[
            vmem((depth, count), BF16),
            vmem((count, cols), BF16),
            vmem((depth, cols), F32),
            dma((depth // 256,)), dma(()), dma((depth // 256,)),
        ],
        compiler_params=pltpu.CompilerParams(vmem_limit_bytes=60 * 2**20),
        name="grad",
    )(nt, slope)


def solution(mesh):
    placed = (P("dp", "mp"), P("mp"), P("mp", "dp"), P("mp", "dp"))
    return jax.shard_map(
        per_device, mesh=mesh, in_specs=placed, out_specs=P("mp", "dp"), check_vma=False
    )
```

```python
import functools
import math

import jax
import jax.numpy as jnp
from jax import lax
from jax.experimental import pallas as pl
from jax.experimental.pallas import tpu as pltpu
from jax.sharding import PartitionSpec as P

FF = 24576
MESH = pl.DeviceIdType.MESH
F32 = jnp.float32
BF16 = jnp.bfloat16


def gelu_slope(value):
    cdf = 0.5 * (1.0 + lax.erf(value * (1.0 / math.sqrt(2.0))))
    dens = jnp.exp(-0.5 * value * value) * (1.0 / math.sqrt(2.0 * math.pi))
    return cdf + value * dens


def remote(src, dst, send_sem, recv_sem, device):
    return pltpu.make_async_remote_copy(
        src_ref=src, dst_ref=dst, send_sem=send_sem, recv_sem=recv_sem,
        device_id=device, device_id_type=MESH,
    )


def slopes_kernel(
    cfg,
    tok_ref, gain_ref, w_hbm, cot_hbm,
    nt_hbm, slope_hbm,
    nt_ref, pre_ref, gs_ref, cot_ref, g_terms, nlocal,
    xs, nall, w, st_part, st_part_in, st_all, own, sendb, recvb,
    g_part, g_part_in, g_all, slope, nb,
    w_sem, c_sem, o_sem, slope_os, z_ss, y_ss, core_ss, x_rs,
    stp_ss, stp_rs, st_ss, st_rs, cot_ss, cot_rs, pre_ss, pre_rs,
    gp_ss, gp_rs, g_ss, g_rs, nb_ss, nb_rs,
    nx, cotx_ss, cotx_rs, nx_ss, nx_rs, sx_ss, sx_rs,
):
    n, m, lines, width_all, token_count = cfg
    rows, depth = tok_ref.shape
    cot_rows, cols = cot_hbm.shape
    chunks, _, chunk = own.shape
    cores = 2
    per_line = n // (lines * cores)
    scale = 1.0 / math.sqrt(token_count)
    me = lax.axis_index("dp")
    my_mp = lax.axis_index("mp")
    core = lax.rem(me, cores)
    across = lax.rem(me // cores, per_line)
    along = me // (cores * per_line)

    group = rows * cores
    near = lines * group
    parts = [(0, near), (near, token_count - near)]

    split = m > 1 and chunk % (128 * m) == 0
    shared = 1 if split else 0
    share = chunk // m if split else chunk

    def share_of(p):
        return pl.ds(pl.multiple_of(p * share, share), share)

    def index(a, b, c):
        return (a * per_line + b) * cores + c

    def dp_peer(k):
        return lax.rem(me + k, n)

    def mp_peer(k):
        return lax.rem(my_mp + k, m)

    w_copy = pltpu.make_async_copy(w_hbm, w, w_sem)
    w_copy.start()
    cot_dst = cot_ref.at[pl.ds(pl.multiple_of(my_mp * cot_rows, cot_rows), cot_rows)]
    cot_copy = pltpu.make_async_copy(cot_hbm, cot_dst, c_sem)
    cot_copy.start()

    barrier = pltpu.get_barrier_semaphore()

    @pl.loop(1, n)
    def _(k):
        pl.semaphore_signal(barrier, inc=1, device_id={"dp": dp_peer(k)}, device_id_type=MESH)

    @pl.loop(1, m)
    def _(k):
        pl.semaphore_signal(barrier, inc=1, device_id={"mp": mp_peer(k)}, device_id_type=MESH)

    values = tok_ref[...].astype(F32)
    lane = lax.broadcasted_iota(jnp.int32, (rows, 128), 1)
    sums = jnp.sum(values, axis=1, keepdims=True)
    squares = jnp.sum(values * values, axis=1, keepdims=True)
    st_part[...] = jnp.where(lane == 0, sums, squares)
    xs[me] = tok_ref[...]

    pl.semaphore_wait(barrier, n + m - 2)

    def line_copy(src_a, up):
        src = index(src_a, across, core)
        to = index(along + 1 if up else along - 1, across, core)
        return remote(xs.at[src], xs.at[src], z_ss.at[int(up), src_a], x_rs.at[src], {"dp": to})

    def across_copy(src_a, j):
        src = index(src_a, across, core)
        to = index(along, lax.rem(across + j, per_line), core)
        return remote(xs.at[src], xs.at[src], y_ss.at[src_a, j], x_rs.at[src], {"dp": to})

    def core_copy(src_a, j):
        src = index(src_a, lax.rem(across + j, per_line), core)
        return remote(xs.at[src], xs.at[src], core_ss.at[src_a, j], x_rs.at[src],
                      {"dp": index(along, across, 1 - core)})

    def arrived(src):
        remote(xs.at[src], xs.at[src], z_ss.at[0, 0], x_rs.at[src], {"dp": dp_peer(1)}).wait_recv()

    by_distance = [(along - s if low else along + s, low) for s in range(1, lines) for low in (True, False)]

    def there(pos, low):
        return pos >= 0 if low else pos < lines

    def can_go(up):
        return along + 1 < lines if up else along > 0

    def across_step(pos):
        for j in range(1, per_line):
            arrived(index(pos, lax.rem(across + j, per_line), core))
            core_copy(pos, j).start()

    def stp_copy(k):
        return remote(st_part, st_part_in.at[my_mp], stp_ss.at[k], stp_rs.at[my_mp],
                      {"mp": mp_peer(k)})

    rest_cols = pl.ds(shared * chunk, cols - shared * chunk)

    def cot_rows_of(p):
        return pl.ds(pl.multiple_of(p * cot_rows, cot_rows), cot_rows)

    def cot_send(k):
        return remote(cot_hbm.at[:, rest_cols], cot_ref.at[cot_rows_of(my_mp), rest_cols],
                      cot_ss.at[k], cot_rs.at[my_mp], {"mp": mp_peer(k)})

    def cot_send_shared(k):
        at = share_of(mp_peer(k))
        return remote(cot_hbm.at[:, at], cot_ref.at[cot_rows_of(my_mp), at],
                      cotx_ss.at[k], cotx_rs.at[my_mp], {"mp": mp_peer(k)})

    for k in range(1, m):
        stp_copy(k).start()
    for k in range(1, m):
        if split:
            cot_send_shared(k).start()
        cot_send(k).start()
    for up in (True, False):
        @pl.when(can_go(up))
        def _():
            line_copy(along, up).start()
    for j in range(1, per_line):
        across_copy(along, j).start()
    core_copy(along, 0).start()

    def relay(pos, low):
        @pl.when(there(pos, low))
        def _():
            arrived(index(pos, across, core))

            @pl.when(can_go(low))
            def _():
                line_copy(pos, low).start()

            for j in range(1, per_line):
                across_copy(pos, j).start()
            core_copy(pos, 0).start()

    for pos, low in by_distance[:2]:
        relay(pos, low)

    total = st_part[...]
    for k in range(1, m):
        p = mp_peer(k)
        remote(st_part, st_part_in.at[p], stp_ss.at[0], stp_rs.at[p], {"mp": p}).wait_recv()
        total = total + st_part_in[p]
    mean = total[:, 0:1] / width_all
    var = total[:, 1:2] / width_all - mean * mean
    st_all[me] = jnp.where(lane == 0, mean, lax.rsqrt(var + 1e-06))

    def st_copy(k):
        return remote(st_all.at[me], st_all.at[me], st_ss.at[k], st_rs.at[me],
                      {"dp": dp_peer(k)})

    @pl.loop(1, n)
    def _(k):
        st_copy(k).start()

    for pos, low in by_distance[2:]:
        relay(pos, low)

    @pl.loop(1, n)
    def _(k):
        p = dp_peer(k)
        remote(st_all.at[p], st_all.at[p], st_ss.at[0], st_rs.at[p], {"dp": p}).wait_recv()

    def normalize(src):
        x = xs[src].astype(F32)
        st = st_all[src]
        value = ((x - st[:, 0:1]) * st[:, 1:2] * gain_ref[...]).astype(BF16)
        nall[pl.ds(pl.multiple_of(src * rows, rows), rows), :] = value
        a = src // (cores * per_line)
        p = lax.rem(lax.rem(src // cores, per_line) + per_line - across, per_line)
        local = ((p * lines + a) * cores + lax.rem(src, cores)) * rows
        nlocal[pl.ds(pl.multiple_of(local, rows), rows), :] = value

    @pl.loop(0, lines)
    def _(k):
        normalize(index(lax.rem(along + k, lines), across, core))

    @pl.loop(0, lines)
    def _(k):
        src = index(lax.rem(along + k, lines), across, 1 - core)
        arrived(src)
        normalize(src)

    w_copy.wait()

    def pre_copy(part, i, k):
        at, size = parts[part]
        return remote(sendb.at[i, pl.ds(at, size)], recvb.at[my_mp, i, pl.ds(at, size)],
                      pre_ss.at[part, i, k], pre_rs.at[part, my_mp, i], {"mp": mp_peer(k)})

    def shared_copy(part, k):
        rows_at = pl.ds(*parts[part])
        at = share_of(mp_peer(k))
        return remote(sendb.at[0, rows_at, at], recvb.at[my_mp, 0, rows_at, at],
                      pre_ss.at[part, 0, k], pre_rs.at[part, my_mp, 0], {"mp": mp_peer(k)})

    def project(part, i, copy=pre_copy):
        at, size = parts[part]
        off = pl.multiple_of(i * chunk, chunk)
        value = jnp.dot(nlocal[pl.ds(at, size), :], w[:, pl.ds(off, chunk)],
                        preferred_element_type=F32)
        own[i, pl.ds(at, size)] = value
        sendb[i, pl.ds(at, size)] = value.astype(BF16)
        for k in range(1, m):
            copy(part, i, k).start()

    def project_first(part):
        if split:
            project(part, 0, lambda part, i, k: shared_copy(part, k))
        else:
            project(part, 0)

    first = 1
    project_first(0)

    across_step(along)
    for pos, low in by_distance:
        @pl.when(there(pos, low))
        def _():
            across_step(pos)

    @pl.loop(first, chunks)
    def _(i):
        project(0, i)

    @pl.loop(0, lines * (per_line - 1))
    def _(i):
        k = i // (per_line - 1)
        j = 1 + lax.rem(i, per_line - 1)
        normalize(index(lax.rem(along + k, lines), lax.rem(across + j, per_line), core))

    @pl.loop(0, lines * (per_line - 1))
    def _(i):
        k = i // (per_line - 1)
        j = 1 + lax.rem(i, per_line - 1)
        src = index(lax.rem(along + k, lines), lax.rem(across + j, per_line), 1 - core)
        arrived(src)
        normalize(src)

    mine = pl.ds(pl.multiple_of(me * rows, rows), rows)
    g_part[...] = lax.dot_general(
        nall[mine, :], nall[...], (((1,), (1,)), ((), ())), preferred_element_type=F32
    )

    def gp_copy(k):
        return remote(g_part, g_part_in.at[my_mp], gp_ss.at[k], gp_rs.at[my_mp],
                      {"mp": mp_peer(k)})

    def g_copy(k):
        return remote(g_all.at[mine], g_all.at[mine], g_ss.at[k], g_rs.at[me],
                      {"dp": dp_peer(k)})

    for k in range(1, m):
        gp_copy(k).start()

    project_first(1)

    @pl.loop(1, chunks)
    def _(i):
        project(1, i)

    gram = g_part[...]
    for k in range(1, m):
        p = mp_peer(k)
        remote(g_part, g_part_in.at[p], gp_ss.at[0], gp_rs.at[p], {"mp": p}).wait_recv()
        gram = gram + g_part_in[p]
    g_all[mine, :] = gram

    @pl.loop(1, n)
    def _(k):
        g_copy(k).start()

    cot_copy.wait()
    for k in range(1, m):
        p = mp_peer(k)
        remote(cot_hbm.at[:, rest_cols], cot_ref.at[cot_rows_of(p), rest_cols],
               cot_ss.at[0], cot_rs.at[p], {"mp": p}).wait_recv()
        if split:
            at = share_of(my_mp)
            remote(cot_hbm.at[:, at], cot_ref.at[cot_rows_of(p), at],
                   cotx_ss.at[0], cotx_rs.at[p], {"mp": p}).wait_recv()

    def local_groups(part):
        at, size = parts[part]
        for g in range(at // group, (at + size) // group):
            p, a = g // lines, g % lines
            row = (a * per_line + lax.rem(across + p, per_line)) * group
            yield pl.ds(pl.multiple_of(row, group), group)

    def first_slopes(part, i, inside, off, width):
        rows_at = pl.ds(*parts[part])
        at = pl.ds(off, width)
        pre = own[i, rows_at, inside]
        for k in range(1, m):
            p = mp_peer(k)
            remote(sendb.at[i, rows_at, inside], recvb.at[p, i, rows_at, inside],
                   pre_ss.at[part, i, 0], pre_rs.at[part, p, i], {"mp": p}).wait_recv()
            pre = pre + recvb[p, i, rows_at, inside].astype(F32)
        cot = jnp.concatenate([cot_ref[r, at] for r in local_groups(part)], axis=0)
        s = (cot.astype(F32) * gelu_slope(pre) * scale).astype(BF16)
        for g, r in enumerate(local_groups(part)):
            pre_ref[r, at] = pre[g * group:(g + 1) * group]
            slope[r, at] = s[g * group:(g + 1) * group]

    mine_off = pl.multiple_of(my_mp * share, share)

    def shared_slopes(part):
        first_slopes(part, 0, share_of(my_mp), mine_off, share)

    def whole_slopes(part, i):
        first_slopes(part, i, pl.ds(0, chunk), pl.multiple_of(i * chunk, chunk), chunk)

    if split:
        shared_slopes(0)

    @pl.loop(shared, chunks)
    def _(i):
        whole_slopes(0, i)

    @pl.loop(1, n)
    def _(k):
        p = dp_peer(k)
        dst = g_all.at[pl.ds(pl.multiple_of(p * rows, rows), rows)]
        remote(dst, dst, g_ss.at[0], g_rs.at[p], {"dp": p}).wait_recv()

    rest = g_all[...]
    for t in range(3):
        term = rest.astype(BF16)
        g_terms[t * token_count:(t + 1) * token_count] = term
        rest = rest - term.astype(F32)

    def ascent(at):
        s = slope[:, at]
        terms = jnp.dot(g_terms[...], s, preferred_element_type=F32)
        t = token_count
        gs = terms[2 * t:] + terms[t:2 * t] + terms[:t]
        gs_ref[:, at] = gs
        return jnp.full((8, 128), jnp.sum(gs * s.astype(F32)), F32)

    def nx_copy(k):
        return remote(nx.at[my_mp], nx.at[my_mp], nx_ss.at[k], nx_rs.at[my_mp],
                      {"mp": mp_peer(k)})

    nb[me] = jnp.zeros_like(nb[me])
    if split:
        shared_slopes(1)
        nx[my_mp] = ascent(pl.ds(mine_off, share))
        for k in range(1, m):
            nx_copy(k).start()

    @pl.loop(shared, chunks)
    def _(i):
        whole_slopes(1, i)
        nb[me] += ascent(pl.ds(pl.multiple_of(i * chunk, chunk), chunk))

    if split:
        for k in range(1, m):
            p = mp_peer(k)
            remote(nx.at[p], nx.at[p], nx_ss.at[0], nx_rs.at[p], {"mp": p}).wait_recv()
        nb[me] += jnp.sum(nx[...], axis=0)

    def nb_copy(k):
        return remote(nb.at[me], nb.at[me], nb_ss.at[k], nb_rs.at[me], {"dp": dp_peer(k)})

    @pl.loop(1, n)
    def _(k):
        nb_copy(k).start()

    @pl.loop(0, depth // 256)
    def _(i):
        off = pl.multiple_of(i * 256, 256)
        nt_ref[pl.ds(off, 256), :] = nall[:, pl.ds(off, 256)].T

    nt_copy = pltpu.make_async_copy(nt_ref, nt_hbm, o_sem.at[0])
    nt_copy.start()

    @pl.loop(1, n)
    def _(k):
        st_copy(k).wait_send()
        g_copy(k).wait_send()

    for pos, low in [(along, True), (along, False)] + by_distance:
        @pl.when(jnp.logical_and(there(pos, low), can_go(low)))
        def _():
            line_copy(pos, low).wait_send()

    @pl.loop(0, lines)
    def _(pos):
        for j in range(per_line):
            core_copy(pos, j).wait_send()
            if j > 0:
                across_copy(pos, j).wait_send()

    for k in range(1, m):
        stp_copy(k).wait_send()
        cot_send(k).wait_send()
        gp_copy(k).wait_send()

        if split:
            cot_send_shared(k).wait_send()
            shared_copy(0, k).wait_send()
            shared_copy(1, k).wait_send()
            nx_copy(k).wait_send()

        @pl.loop(shared, chunks)
        def _(i):
            pre_copy(0, i, k).wait_send()
            pre_copy(1, i, k).wait_send()

    @pl.loop(1, n)
    def _(k):
        p = dp_peer(k)
        remote(nb.at[p], nb.at[p], nb_ss.at[0], nb_rs.at[p], {"dp": p}).wait_recv()
        nb_copy(k).wait_send()

    squared = jnp.sum(nb[...], axis=0)[0:1, 0:1]
    size = jnp.sqrt(jnp.maximum(squared, 0.0)) + 1e-12
    radius = 0.5 * math.sqrt(FF)

    def slope_copy(i):
        at = pl.ds(pl.multiple_of(i * chunk, chunk), chunk)
        return pltpu.make_async_copy(slope.at[:, at], slope_hbm.at[:, at], slope_os.at[i])

    def second_slopes(at):
        pre = pre_ref[:, at] + radius * gs_ref[:, at] / size
        slope[:, at] = (cot_ref[:, at].astype(F32) * gelu_slope(pre) * scale).astype(BF16)

    def sx_copy(k):
        at = pl.ds(mine_off, share)
        return remote(slope.at[:, at], slope.at[:, at], sx_ss.at[k], sx_rs.at[my_mp],
                      {"mp": mp_peer(k)})

    if split:
        second_slopes(pl.ds(mine_off, share))
        for k in range(1, m):
            sx_copy(k).start()

    @pl.loop(shared, chunks)
    def _(i):
        second_slopes(pl.ds(pl.multiple_of(i * chunk, chunk), chunk))
        slope_copy(i).start()

    if split:
        for k in range(1, m):
            p = mp_peer(k)
            at = share_of(p)
            remote(slope.at[:, at], slope.at[:, at], sx_ss.at[0], sx_rs.at[p], {"mp": p}).wait_recv()
        slope_copy(0).start()
        for k in range(1, m):
            sx_copy(k).wait_send()

    nt_copy.wait()

    @pl.loop(0, chunks)
    def _(i):
        slope_copy(i).wait()


def grad_kernel(nt_hbm, slope_hbm, out_hbm, nt, slope, out, nt_sem, slope_sem, out_sem):
    blocks = nt_sem.shape[0]
    rows = nt.shape[0] // blocks

    def cut(i):
        return pl.ds(pl.multiple_of(i * rows, rows), rows)

    def nt_copy(i):
        return pltpu.make_async_copy(nt_hbm.at[cut(i)], nt.at[cut(i)], nt_sem.at[i])

    def out_copy(i):
        return pltpu.make_async_copy(out.at[cut(i)], out_hbm.at[cut(i)], out_sem.at[i])

    slope_copy = pltpu.make_async_copy(slope_hbm, slope, slope_sem)
    slope_copy.start()

    @pl.loop(0, blocks)
    def _(i):
        nt_copy(i).start()

    slope_copy.wait()

    @pl.loop(0, blocks)
    def _(i):
        nt_copy(i).wait()
        out[cut(i), :] = jnp.dot(nt[cut(i), :], slope[...], preferred_element_type=F32)
        out_copy(i).start()

    @pl.loop(0, blocks)
    def _(i):
        out_copy(i).wait()


def per_device(tokens, norm_gain, w_up, cotangent):
    n, m = lax.axis_size("dp"), lax.axis_size("mp")
    rows, depth = tokens.shape
    count = rows * n
    cols = w_up.shape[1]
    lines = 4
    chunk = next(c for c in (512, 256, 128) if cols % c == 0)
    chunks = cols // chunk
    per_line = n // (2 * lines)
    cot_rows = cotangent.shape[0]
    dma, vmem = pltpu.SemaphoreType.DMA, pltpu.VMEM
    whole = pl.BlockSpec(memory_space=pltpu.VMEM)
    hbm = pl.BlockSpec(memory_space=pl.ANY)
    cfg = (n, m, lines, depth * m, count)
    nt, slope = pl.pallas_call(
        functools.partial(slopes_kernel, cfg),
        out_shape=(
            jax.ShapeDtypeStruct((depth, count), BF16),
            jax.ShapeDtypeStruct((count, cols), BF16),
        ),
        in_specs=[whole, whole, hbm, hbm],
        out_specs=[hbm] * 2,
        scratch_shapes=[
            vmem((depth, count), BF16),
            vmem((count, cols), F32),
            vmem((count, cols), F32),
            vmem((count, cols), BF16),
            vmem((3 * count, count), BF16),
            vmem((count, depth), BF16),
            vmem((n, rows, depth), BF16),
            vmem((count, depth), BF16),
            vmem((depth, cols), BF16),
            vmem((rows, 128), F32),
            vmem((m, rows, 128), F32),
            vmem((n, rows, 128), F32),
            vmem((chunks, count, chunk), F32),
            vmem((chunks, count, chunk), BF16),
            vmem((m, chunks, count, chunk), BF16),
            vmem((rows, count), F32),
            vmem((m, rows, count), F32),
            vmem((count, count), F32),
            vmem((count, cols), BF16),
            vmem((n, 8, 128), F32),
            dma(()), dma(()), dma((1,)), dma((chunks,)),
            dma((2, lines)), dma((lines, per_line)), dma((lines, per_line)),
            dma((n,)),
            dma((m,)), dma((m,)), dma((n,)), dma((n,)), dma((m,)), dma((m,)),
            dma((2, chunks, m)), dma((2, m, chunks)),
            dma((m,)), dma((m,)), dma((n,)), dma((n,)), dma((n,)), dma((n,)),
            vmem((m, 8, 128), F32),
            dma((m,)), dma((m,)), dma((m,)), dma((m,)), dma((m,)), dma((m,)),
        ],
        compiler_params=pltpu.CompilerParams(
            collective_id=0, has_side_effects=True, vmem_limit_bytes=56 * 2**20
        ),
        name="slopes",
    )(tokens, norm_gain.reshape(1, depth), w_up, cotangent)

    return pl.pallas_call(
        grad_kernel,
        out_shape=jax.ShapeDtypeStruct((depth, cols), F32),
        in_specs=[hbm, hbm],
        out_specs=hbm,
        scratch_shapes=[
            vmem((depth, count), BF16),
            vmem((count, cols), BF16),
            vmem((depth, cols), F32),
            dma((depth // 256,)), dma(()), dma((depth // 256,)),
        ],
        compiler_params=pltpu.CompilerParams(vmem_limit_bytes=60 * 2**20),
        name="grad",
    )(nt, slope)


def solution(mesh):
    placed = (P("dp", "mp"), P("mp"), P("mp", "dp"), P("mp", "dp"))
    return jax.shard_map(
        per_device, mesh=mesh, in_specs=placed, out_specs=P("mp", "dp"), check_vma=False
    )
```

```python
import functools
import math

import jax
import jax.numpy as jnp
from jax import lax
from jax.experimental import pallas as pl
from jax.experimental.pallas import tpu as pltpu
from jax.sharding import PartitionSpec as P

FF = 24576
MESH = pl.DeviceIdType.MESH
F32 = jnp.float32
BF16 = jnp.bfloat16


def gelu_slope(value):
    cdf = 0.5 * (1.0 + lax.erf(value * (1.0 / math.sqrt(2.0))))
    dens = jnp.exp(-0.5 * value * value) * (1.0 / math.sqrt(2.0 * math.pi))
    return cdf + value * dens


def remote(src, dst, send_sem, recv_sem, device):
    return pltpu.make_async_remote_copy(
        src_ref=src, dst_ref=dst, send_sem=send_sem, recv_sem=recv_sem,
        device_id=device, device_id_type=MESH,
    )


def slopes_kernel(
    cfg,
    tok_ref, gain_ref, w_hbm, cot_hbm,
    nt_hbm, pre_hbm, gs_hbm, cot_out, norm_ref,
    nt_ref, pre_ref, gs_ref, cot_ref, g_terms, nlocal,
    xs, nall, w, st_part, st_part_in, st_all, own, sendb, recvb,
    g_part, g_part_in, g_all, slope, nb,
    w_sem, c_sem, o_sem, pre_os, gs_os, z_ss, y_ss, core_ss, x_rs,
    stp_ss, stp_rs, st_ss, st_rs, cot_ss, cot_rs, pre_ss, pre_rs,
    gp_ss, gp_rs, g_ss, g_rs, nb_ss, nb_rs,
):
    n, m, lines, width_all, token_count = cfg
    rows, depth = tok_ref.shape
    cot_rows, cols = cot_hbm.shape
    chunks, _, chunk = own.shape
    cores = 2
    per_line = n // (lines * cores)
    scale = 1.0 / math.sqrt(token_count)
    me = lax.axis_index("dp")
    my_mp = lax.axis_index("mp")
    core = lax.rem(me, cores)
    across = lax.rem(me // cores, per_line)
    along = me // (cores * per_line)

    group = rows * cores
    near = lines * group
    parts = [(0, near), (near, token_count - near)]

    def index(a, b, c):
        return (a * per_line + b) * cores + c

    def dp_peer(k):
        return lax.rem(me + k, n)

    def mp_peer(k):
        return lax.rem(my_mp + k, m)

    w_copy = pltpu.make_async_copy(w_hbm, w, w_sem)
    w_copy.start()
    cot_dst = cot_ref.at[pl.ds(pl.multiple_of(my_mp * cot_rows, cot_rows), cot_rows)]
    cot_copy = pltpu.make_async_copy(cot_hbm, cot_dst, c_sem)
    cot_copy.start()

    barrier = pltpu.get_barrier_semaphore()

    @pl.loop(1, n)
    def _(k):
        pl.semaphore_signal(barrier, inc=1, device_id={"dp": dp_peer(k)}, device_id_type=MESH)

    @pl.loop(1, m)
    def _(k):
        pl.semaphore_signal(barrier, inc=1, device_id={"mp": mp_peer(k)}, device_id_type=MESH)

    values = tok_ref[...].astype(F32)
    lane = lax.broadcasted_iota(jnp.int32, (rows, 128), 1)
    sums = jnp.sum(values, axis=1, keepdims=True)
    squares = jnp.sum(values * values, axis=1, keepdims=True)
    st_part[...] = jnp.where(lane == 0, sums, squares)
    xs[me] = tok_ref[...]

    pl.semaphore_wait(barrier, n + m - 2)

    def line_copy(src_a, up):
        src = index(src_a, across, core)
        to = index(along + 1 if up else along - 1, across, core)
        return remote(xs.at[src], xs.at[src], z_ss.at[int(up), src_a], x_rs.at[src], {"dp": to})

    def across_copy(src_a, j):
        src = index(src_a, across, core)
        to = index(along, lax.rem(across + j, per_line), core)
        return remote(xs.at[src], xs.at[src], y_ss.at[src_a, j], x_rs.at[src], {"dp": to})

    def core_copy(src_a, j):
        src = index(src_a, lax.rem(across + j, per_line), core)
        return remote(xs.at[src], xs.at[src], core_ss.at[src_a, j], x_rs.at[src],
                      {"dp": index(along, across, 1 - core)})

    def arrived(src):
        remote(xs.at[src], xs.at[src], z_ss.at[0, 0], x_rs.at[src], {"dp": dp_peer(1)}).wait_recv()

    by_distance = [(along - s if low else along + s, low) for s in range(1, lines) for low in (True, False)]

    def there(pos, low):
        return pos >= 0 if low else pos < lines

    def can_go(up):
        return along + 1 < lines if up else along > 0

    def across_step(pos):
        for j in range(1, per_line):
            arrived(index(pos, lax.rem(across + j, per_line), core))
            core_copy(pos, j).start()

    def stp_copy(k):
        return remote(st_part, st_part_in.at[my_mp], stp_ss.at[k], stp_rs.at[my_mp],
                      {"mp": mp_peer(k)})

    def cot_send(k):
        return remote(cot_hbm, cot_dst, cot_ss.at[k], cot_rs.at[my_mp], {"mp": mp_peer(k)})

    for k in range(1, m):
        stp_copy(k).start()
    for k in range(1, m):
        cot_send(k).start()
    for up in (True, False):
        @pl.when(can_go(up))
        def _():
            line_copy(along, up).start()
    for j in range(1, per_line):
        across_copy(along, j).start()
    core_copy(along, 0).start()

    def relay(pos, low):
        @pl.when(there(pos, low))
        def _():
            arrived(index(pos, across, core))

            @pl.when(can_go(low))
            def _():
                line_copy(pos, low).start()

            for j in range(1, per_line):
                across_copy(pos, j).start()
            core_copy(pos, 0).start()

    for pos, low in by_distance[:2]:
        relay(pos, low)

    total = st_part[...]
    for k in range(1, m):
        p = mp_peer(k)
        remote(st_part, st_part_in.at[p], stp_ss.at[0], stp_rs.at[p], {"mp": p}).wait_recv()
        total = total + st_part_in[p]
    mean = total[:, 0:1] / width_all
    var = total[:, 1:2] / width_all - mean * mean
    st_all[me] = jnp.where(lane == 0, mean, lax.rsqrt(var + 1e-06))

    def st_copy(k):
        return remote(st_all.at[me], st_all.at[me], st_ss.at[k], st_rs.at[me],
                      {"dp": dp_peer(k)})

    @pl.loop(1, n)
    def _(k):
        st_copy(k).start()

    for pos, low in by_distance[2:]:
        relay(pos, low)

    @pl.loop(1, n)
    def _(k):
        p = dp_peer(k)
        remote(st_all.at[p], st_all.at[p], st_ss.at[0], st_rs.at[p], {"dp": p}).wait_recv()

    def normalize(src):
        x = xs[src].astype(F32)
        st = st_all[src]
        value = ((x - st[:, 0:1]) * st[:, 1:2] * gain_ref[...]).astype(BF16)
        nall[pl.ds(pl.multiple_of(src * rows, rows), rows), :] = value
        a = src // (cores * per_line)
        p = lax.rem(lax.rem(src // cores, per_line) + per_line - across, per_line)
        local = ((p * lines + a) * cores + lax.rem(src, cores)) * rows
        nlocal[pl.ds(pl.multiple_of(local, rows), rows), :] = value

    @pl.loop(0, lines)
    def _(k):
        normalize(index(lax.rem(along + k, lines), across, core))

    @pl.loop(0, lines)
    def _(k):
        src = index(lax.rem(along + k, lines), across, 1 - core)
        arrived(src)
        normalize(src)

    w_copy.wait()

    def pre_copy(part, i, k):
        at, size = parts[part]
        return remote(sendb.at[i, pl.ds(at, size)], recvb.at[my_mp, i, pl.ds(at, size)],
                      pre_ss.at[part, i, k], pre_rs.at[part, my_mp, i], {"mp": mp_peer(k)})

    def project(part, i):
        at, size = parts[part]
        off = pl.multiple_of(i * chunk, chunk)
        value = jnp.dot(nlocal[pl.ds(at, size), :], w[:, pl.ds(off, chunk)],
                        preferred_element_type=F32)
        own[i, pl.ds(at, size)] = value
        sendb[i, pl.ds(at, size)] = value.astype(BF16)
        for k in range(1, m):
            pre_copy(part, i, k).start()

    first = 1

    @pl.loop(0, first)
    def _(i):
        project(0, i)

    across_step(along)
    for pos, low in by_distance:
        @pl.when(there(pos, low))
        def _():
            across_step(pos)

    @pl.loop(first, chunks)
    def _(i):
        project(0, i)

    @pl.loop(0, lines * (per_line - 1))
    def _(i):
        k = i // (per_line - 1)
        j = 1 + lax.rem(i, per_line - 1)
        normalize(index(lax.rem(along + k, lines), lax.rem(across + j, per_line), core))

    @pl.loop(0, lines * (per_line - 1))
    def _(i):
        k = i // (per_line - 1)
        j = 1 + lax.rem(i, per_line - 1)
        src = index(lax.rem(along + k, lines), lax.rem(across + j, per_line), 1 - core)
        arrived(src)
        normalize(src)

    mine = pl.ds(pl.multiple_of(me * rows, rows), rows)
    g_part[...] = lax.dot_general(
        nall[mine, :], nall[...], (((1,), (1,)), ((), ())), preferred_element_type=F32
    )

    def gp_copy(k):
        return remote(g_part, g_part_in.at[my_mp], gp_ss.at[k], gp_rs.at[my_mp],
                      {"mp": mp_peer(k)})

    def g_copy(k):
        return remote(g_all.at[mine], g_all.at[mine], g_ss.at[k], g_rs.at[me],
                      {"dp": dp_peer(k)})

    for k in range(1, m):
        gp_copy(k).start()

    @pl.loop(0, chunks)
    def _(i):
        project(1, i)

    gram = g_part[...]
    for k in range(1, m):
        p = mp_peer(k)
        remote(g_part, g_part_in.at[p], gp_ss.at[0], gp_rs.at[p], {"mp": p}).wait_recv()
        gram = gram + g_part_in[p]
    g_all[mine, :] = gram

    @pl.loop(1, n)
    def _(k):
        g_copy(k).start()

    cot_copy.wait()
    for k in range(1, m):
        p = mp_peer(k)
        dst = cot_ref.at[pl.ds(pl.multiple_of(p * cot_rows, cot_rows), cot_rows)]
        remote(cot_hbm, dst, cot_ss.at[0], cot_rs.at[p], {"mp": p}).wait_recv()

    cot_write = pltpu.make_async_copy(cot_ref, cot_out, o_sem.at[1])
    cot_write.start()

    def out_copy(i, buf, dst, sem):
        at = pl.ds(pl.multiple_of(i * chunk, chunk), chunk)
        return pltpu.make_async_copy(buf.at[:, at], dst.at[:, at], sem.at[i])

    def local_groups(part):
        at, size = parts[part]
        for g in range(at // group, (at + size) // group):
            p, a = g // lines, g % lines
            row = (a * per_line + lax.rem(across + p, per_line)) * group
            yield pl.ds(pl.multiple_of(row, group), group)

    def first_slopes(part, i):
        at, size = parts[part]
        off = pl.multiple_of(i * chunk, chunk)
        pre = own[i, pl.ds(at, size)]
        for k in range(1, m):
            p = mp_peer(k)
            remote(sendb.at[i, pl.ds(at, size)], recvb.at[p, i, pl.ds(at, size)],
                   pre_ss.at[part, i, 0], pre_rs.at[part, p, i], {"mp": p}).wait_recv()
            pre = pre + recvb[p, i, pl.ds(at, size)].astype(F32)
        cot = jnp.concatenate([cot_ref[r, pl.ds(off, chunk)] for r in local_groups(part)], axis=0)
        s = (cot.astype(F32) * gelu_slope(pre) * scale).astype(BF16)
        for g, r in enumerate(local_groups(part)):
            pre_ref[r, pl.ds(off, chunk)] = pre[g * group:(g + 1) * group]
            slope[r, pl.ds(off, chunk)] = s[g * group:(g + 1) * group]

    @pl.loop(0, chunks)
    def _(i):
        first_slopes(0, i)

    @pl.loop(1, n)
    def _(k):
        p = dp_peer(k)
        dst = g_all.at[pl.ds(pl.multiple_of(p * rows, rows), rows)]
        remote(dst, dst, g_ss.at[0], g_rs.at[p], {"dp": p}).wait_recv()

    rest = g_all[...]
    for t in range(3):
        term = rest.astype(BF16)
        g_terms[t * token_count:(t + 1) * token_count] = term
        rest = rest - term.astype(F32)

    nb[me] = jnp.zeros_like(nb[me])

    @pl.loop(0, chunks)
    def _(i):
        first_slopes(1, i)
        out_copy(i, pre_ref, pre_hbm, pre_os).start()
        off = pl.multiple_of(i * chunk, chunk)
        s = slope[:, pl.ds(off, chunk)]
        terms = jnp.dot(g_terms[...], s, preferred_element_type=F32)
        t = token_count
        gs = terms[2 * t:] + terms[t:2 * t] + terms[:t]
        gs_ref[:, pl.ds(off, chunk)] = gs
        out_copy(i, gs_ref, gs_hbm, gs_os).start()
        nb[me] += jnp.full((8, 128), jnp.sum(gs * s.astype(F32)), F32)

    def nb_copy(k):
        return remote(nb.at[me], nb.at[me], nb_ss.at[k], nb_rs.at[me], {"dp": dp_peer(k)})

    @pl.loop(1, n)
    def _(k):
        nb_copy(k).start()

    @pl.loop(0, depth // 256)
    def _(i):
        off = pl.multiple_of(i * 256, 256)
        nt_ref[pl.ds(off, 256), :] = nall[:, pl.ds(off, 256)].T

    nt_copy = pltpu.make_async_copy(nt_ref, nt_hbm, o_sem.at[0])
    nt_copy.start()

    @pl.loop(1, n)
    def _(k):
        st_copy(k).wait_send()
        g_copy(k).wait_send()

    for pos, low in [(along, True), (along, False)] + by_distance:
        @pl.when(jnp.logical_and(there(pos, low), can_go(low)))
        def _():
            line_copy(pos, low).wait_send()

    @pl.loop(0, lines)
    def _(pos):
        for j in range(per_line):
            core_copy(pos, j).wait_send()
            if j > 0:
                across_copy(pos, j).wait_send()

    for k in range(1, m):
        stp_copy(k).wait_send()
        cot_send(k).wait_send()
        gp_copy(k).wait_send()

        @pl.loop(0, chunks)
        def _(i):
            pre_copy(0, i, k).wait_send()
            pre_copy(1, i, k).wait_send()

    @pl.loop(1, n)
    def _(k):
        p = dp_peer(k)
        remote(nb.at[p], nb.at[p], nb_ss.at[0], nb_rs.at[p], {"dp": p}).wait_recv()
        nb_copy(k).wait_send()

    norm_ref[...] = jnp.sum(nb[...], axis=0)
    nt_copy.wait()
    cot_write.wait()

    @pl.loop(0, chunks)
    def _(i):
        out_copy(i, pre_ref, pre_hbm, pre_os).wait()
        out_copy(i, gs_ref, gs_hbm, gs_os).wait()


def grad_kernel(
    token_count, norm_ref, nt_hbm, pre_hbm, gs_hbm, cot_hbm, out_hbm,
    nt, pre, gs, cot, slope, out, nt_sem, in_sem, out_sem,
):
    chunks, blocks = out_sem.shape
    rows = nt.shape[0] // blocks
    narrow = slope.shape[1]

    def down(i):
        return pl.ds(pl.multiple_of(i * rows, rows), rows)

    def inputs(j):
        at = pl.ds(j * narrow, narrow)
        pairs = ((pre_hbm, pre), (gs_hbm, gs), (cot_hbm, cot))
        return [
            pltpu.make_async_copy(src.at[:, at], dst.at[:, at], in_sem.at[k, j])
            for k, (src, dst) in enumerate(pairs)
        ]

    def nt_copy(i):
        return pltpu.make_async_copy(nt_hbm.at[down(i)], nt.at[down(i)], nt_sem.at[i])

    def out_copy(i, j):
        at = pl.ds(j * narrow, narrow)
        return pltpu.make_async_copy(out.at[down(i), at], out_hbm.at[down(i), at], out_sem.at[j, i])

    for copy in inputs(0):
        copy.start()

    @pl.loop(0, blocks)
    def _(i):
        nt_copy(i).start()

    for j in range(1, chunks):
        for copy in inputs(j):
            copy.start()

    scale = 1.0 / math.sqrt(token_count)
    size = jnp.sqrt(jnp.maximum(norm_ref[0:1, 0:1], 0.0)) + 1e-12
    radius = 0.5 * math.sqrt(FF)
    for j in range(chunks):
        at = pl.ds(j * narrow, narrow)
        for copy in inputs(j):
            copy.wait()
        perturbed = pre[:, at] + radius * gs[:, at] / size
        slope[...] = (cot[:, at].astype(F32) * gelu_slope(perturbed) * scale).astype(BF16)

        @pl.loop(0, blocks)
        def _(i):
            if j == 0:
                nt_copy(i).wait()
            out[down(i), at] = jnp.dot(nt[down(i), :], slope[...], preferred_element_type=F32)
            out_copy(i, j).start()

    for j in range(chunks):
        @pl.loop(0, blocks)
        def _(i):
            out_copy(i, j).wait()


def per_device(tokens, norm_gain, w_up, cotangent):
    n, m = lax.axis_size("dp"), lax.axis_size("mp")
    rows, depth = tokens.shape
    count = rows * n
    cols = w_up.shape[1]
    lines = 4
    chunk = next(c for c in (512, 256, 128) if cols % c == 0)
    chunks = cols // chunk
    per_line = n // (2 * lines)
    narrow = min(chunk, 256)
    blocks = next(b for b in (4, 2, 1) if depth % (b * 16) == 0)
    cot_rows = cotangent.shape[0]
    dma, vmem = pltpu.SemaphoreType.DMA, pltpu.VMEM
    whole = pl.BlockSpec(memory_space=pltpu.VMEM)
    hbm = pl.BlockSpec(memory_space=pl.ANY)
    cfg = (n, m, lines, depth * m, count)
    nt, pre, gs, cot, norm = pl.pallas_call(
        functools.partial(slopes_kernel, cfg),
        out_shape=(
            jax.ShapeDtypeStruct((depth, count), BF16),
            jax.ShapeDtypeStruct((count, cols), F32),
            jax.ShapeDtypeStruct((count, cols), F32),
            jax.ShapeDtypeStruct((count, cols), BF16),
            jax.ShapeDtypeStruct((8, 128), F32),
        ),
        in_specs=[whole, whole, hbm, hbm],
        out_specs=[hbm] * 4 + [whole],
        scratch_shapes=[
            vmem((depth, count), BF16),
            vmem((count, cols), F32),
            vmem((count, cols), F32),
            vmem((count, cols), BF16),
            vmem((3 * count, count), BF16),
            vmem((count, depth), BF16),
            vmem((n, rows, depth), BF16),
            vmem((count, depth), BF16),
            vmem((depth, cols), BF16),
            vmem((rows, 128), F32),
            vmem((m, rows, 128), F32),
            vmem((n, rows, 128), F32),
            vmem((chunks, count, chunk), F32),
            vmem((chunks, count, chunk), BF16),
            vmem((m, chunks, count, chunk), BF16),
            vmem((rows, count), F32),
            vmem((m, rows, count), F32),
            vmem((count, count), F32),
            vmem((count, cols), BF16),
            vmem((n, 8, 128), F32),
            dma(()), dma(()), dma((2,)), dma((chunks,)), dma((chunks,)),
            dma((2, lines)), dma((lines, per_line)), dma((lines, per_line)),
            dma((n,)),
            dma((m,)), dma((m,)), dma((n,)), dma((n,)), dma((m,)), dma((m,)),
            dma((2, chunks, m)), dma((2, m, chunks)),
            dma((m,)), dma((m,)), dma((n,)), dma((n,)), dma((n,)), dma((n,)),
        ],
        compiler_params=pltpu.CompilerParams(
            collective_id=0, has_side_effects=True, vmem_limit_bytes=56 * 2**20
        ),
        name="slopes",
    )(tokens, norm_gain.reshape(1, depth), w_up, cotangent)

    return pl.pallas_call(
        functools.partial(grad_kernel, count),
        out_shape=jax.ShapeDtypeStruct((depth, cols), F32),
        in_specs=[whole] + [hbm] * 4,
        out_specs=hbm,
        scratch_shapes=[
            vmem((depth, count), BF16),
            vmem((count, cols), F32),
            vmem((count, cols), F32),
            vmem((count, cols), BF16),
            vmem((count, narrow), BF16),
            vmem((depth, cols), F32),
            dma((blocks,)), dma((3, cols // narrow)), dma((cols // narrow, blocks)),
        ],
        compiler_params=pltpu.CompilerParams(vmem_limit_bytes=60 * 2**20),
        name="grad",
    )(norm, nt, pre, gs, cot)


def solution(mesh):
    placed = (P("dp", "mp"), P("mp"), P("mp", "dp"), P("mp", "dp"))
    return jax.shard_map(
        per_device, mesh=mesh, in_specs=placed, out_specs=P("mp", "dp"), check_vma=False
    )
```

```python
import functools
import math

import jax
import jax.numpy as jnp
from jax import lax
from jax.experimental import pallas as pl
from jax.experimental.pallas import tpu as pltpu
from jax.sharding import PartitionSpec as P

FF = 24576
MESH = pl.DeviceIdType.MESH
F32 = jnp.float32
BF16 = jnp.bfloat16


def gelu_slope(value):
    cdf = 0.5 * (1.0 + lax.erf(value * (1.0 / math.sqrt(2.0))))
    dens = jnp.exp(-0.5 * value * value) * (1.0 / math.sqrt(2.0 * math.pi))
    return cdf + value * dens


def remote(src, dst, send_sem, recv_sem, device):
    return pltpu.make_async_remote_copy(
        src_ref=src, dst_ref=dst, send_sem=send_sem, recv_sem=recv_sem,
        device_id=device, device_id_type=MESH,
    )


def slopes_kernel(
    cfg,
    tok_ref, gain_ref, w_hbm, cot_hbm,
    nt_hbm, slope_hbm,
    nt_ref, pre_ref, gs_ref, cot_ref, g_terms, nlocal,
    xs, nall, w, st_part, st_part_in, st_all, own, sendb, recvb,
    g_part, g_part_in, g_all, slope, nb,
    w_sem, c_sem, o_sem, slope_os, z_ss, y_ss, core_ss, x_rs,
    stp_ss, stp_rs, st_ss, st_rs, cot_ss, cot_rs, pre_ss, pre_rs,
    gp_ss, gp_rs, g_ss, g_rs, nb_ss, nb_rs,
):
    n, m, lines, width_all, token_count = cfg
    rows, depth = tok_ref.shape
    cot_rows, cols = cot_hbm.shape
    chunks, _, chunk = own.shape
    cores = 2
    per_line = n // (lines * cores)
    scale = 1.0 / math.sqrt(token_count)
    me = lax.axis_index("dp")
    my_mp = lax.axis_index("mp")
    core = lax.rem(me, cores)
    across = lax.rem(me // cores, per_line)
    along = me // (cores * per_line)

    group = rows * cores
    near = lines * group
    parts = [(0, near), (near, token_count - near)]

    def index(a, b, c):
        return (a * per_line + b) * cores + c

    def dp_peer(k):
        return lax.rem(me + k, n)

    def mp_peer(k):
        return lax.rem(my_mp + k, m)

    w_copy = pltpu.make_async_copy(w_hbm, w, w_sem)
    w_copy.start()
    cot_dst = cot_ref.at[pl.ds(pl.multiple_of(my_mp * cot_rows, cot_rows), cot_rows)]
    cot_copy = pltpu.make_async_copy(cot_hbm, cot_dst, c_sem)
    cot_copy.start()

    barrier = pltpu.get_barrier_semaphore()

    @pl.loop(1, n)
    def _(k):
        pl.semaphore_signal(barrier, inc=1, device_id={"dp": dp_peer(k)}, device_id_type=MESH)

    @pl.loop(1, m)
    def _(k):
        pl.semaphore_signal(barrier, inc=1, device_id={"mp": mp_peer(k)}, device_id_type=MESH)

    values = tok_ref[...].astype(F32)
    lane = lax.broadcasted_iota(jnp.int32, (rows, 128), 1)
    sums = jnp.sum(values, axis=1, keepdims=True)
    squares = jnp.sum(values * values, axis=1, keepdims=True)
    st_part[...] = jnp.where(lane == 0, sums, squares)
    xs[me] = tok_ref[...]

    pl.semaphore_wait(barrier, n + m - 2)

    def line_copy(src_a, up):
        src = index(src_a, across, core)
        to = index(along + 1 if up else along - 1, across, core)
        return remote(xs.at[src], xs.at[src], z_ss.at[int(up), src_a], x_rs.at[src], {"dp": to})

    def across_copy(src_a, j):
        src = index(src_a, across, core)
        to = index(along, lax.rem(across + j, per_line), core)
        return remote(xs.at[src], xs.at[src], y_ss.at[src_a, j], x_rs.at[src], {"dp": to})

    def core_copy(src_a, j):
        src = index(src_a, lax.rem(across + j, per_line), core)
        return remote(xs.at[src], xs.at[src], core_ss.at[src_a, j], x_rs.at[src],
                      {"dp": index(along, across, 1 - core)})

    def arrived(src):
        remote(xs.at[src], xs.at[src], z_ss.at[0, 0], x_rs.at[src], {"dp": dp_peer(1)}).wait_recv()

    by_distance = [(along - s if low else along + s, low) for s in range(1, lines) for low in (True, False)]

    def there(pos, low):
        return pos >= 0 if low else pos < lines

    def can_go(up):
        return along + 1 < lines if up else along > 0

    def across_step(pos):
        for j in range(1, per_line):
            arrived(index(pos, lax.rem(across + j, per_line), core))
            core_copy(pos, j).start()

    def stp_copy(k):
        return remote(st_part, st_part_in.at[my_mp], stp_ss.at[k], stp_rs.at[my_mp],
                      {"mp": mp_peer(k)})

    def cot_send(k):
        return remote(cot_hbm, cot_dst, cot_ss.at[k], cot_rs.at[my_mp], {"mp": mp_peer(k)})

    for k in range(1, m):
        stp_copy(k).start()
    for k in range(1, m):
        cot_send(k).start()
    for up in (True, False):
        @pl.when(can_go(up))
        def _():
            line_copy(along, up).start()
    for j in range(1, per_line):
        across_copy(along, j).start()
    core_copy(along, 0).start()

    def relay(pos, low):
        @pl.when(there(pos, low))
        def _():
            arrived(index(pos, across, core))

            @pl.when(can_go(low))
            def _():
                line_copy(pos, low).start()

            for j in range(1, per_line):
                across_copy(pos, j).start()
            core_copy(pos, 0).start()

    for pos, low in by_distance[:2]:
        relay(pos, low)

    total = st_part[...]
    for k in range(1, m):
        p = mp_peer(k)
        remote(st_part, st_part_in.at[p], stp_ss.at[0], stp_rs.at[p], {"mp": p}).wait_recv()
        total = total + st_part_in[p]
    mean = total[:, 0:1] / width_all
    var = total[:, 1:2] / width_all - mean * mean
    st_all[me] = jnp.where(lane == 0, mean, lax.rsqrt(var + 1e-06))

    def st_copy(k):
        return remote(st_all.at[me], st_all.at[me], st_ss.at[k], st_rs.at[me],
                      {"dp": dp_peer(k)})

    @pl.loop(1, n)
    def _(k):
        st_copy(k).start()

    for pos, low in by_distance[2:]:
        relay(pos, low)

    @pl.loop(1, n)
    def _(k):
        p = dp_peer(k)
        remote(st_all.at[p], st_all.at[p], st_ss.at[0], st_rs.at[p], {"dp": p}).wait_recv()

    def normalize(src):
        x = xs[src].astype(F32)
        st = st_all[src]
        value = ((x - st[:, 0:1]) * st[:, 1:2] * gain_ref[...]).astype(BF16)
        nall[pl.ds(pl.multiple_of(src * rows, rows), rows), :] = value
        a = src // (cores * per_line)
        p = lax.rem(lax.rem(src // cores, per_line) + per_line - across, per_line)
        local = ((p * lines + a) * cores + lax.rem(src, cores)) * rows
        nlocal[pl.ds(pl.multiple_of(local, rows), rows), :] = value

    @pl.loop(0, lines)
    def _(k):
        normalize(index(lax.rem(along + k, lines), across, core))

    @pl.loop(0, lines)
    def _(k):
        src = index(lax.rem(along + k, lines), across, 1 - core)
        arrived(src)
        normalize(src)

    w_copy.wait()

    def pre_copy(part, i, k):
        at, size = parts[part]
        return remote(sendb.at[i, pl.ds(at, size)], recvb.at[my_mp, i, pl.ds(at, size)],
                      pre_ss.at[part, i, k], pre_rs.at[part, my_mp, i], {"mp": mp_peer(k)})

    def project(part, i):
        at, size = parts[part]
        off = pl.multiple_of(i * chunk, chunk)
        value = jnp.dot(nlocal[pl.ds(at, size), :], w[:, pl.ds(off, chunk)],
                        preferred_element_type=F32)
        own[i, pl.ds(at, size)] = value
        sendb[i, pl.ds(at, size)] = value.astype(BF16)
        for k in range(1, m):
            pre_copy(part, i, k).start()

    first = 1

    @pl.loop(0, first)
    def _(i):
        project(0, i)

    across_step(along)
    for pos, low in by_distance:
        @pl.when(there(pos, low))
        def _():
            across_step(pos)

    @pl.loop(first, chunks)
    def _(i):
        project(0, i)

    @pl.loop(0, lines * (per_line - 1))
    def _(i):
        k = i // (per_line - 1)
        j = 1 + lax.rem(i, per_line - 1)
        normalize(index(lax.rem(along + k, lines), lax.rem(across + j, per_line), core))

    @pl.loop(0, lines * (per_line - 1))
    def _(i):
        k = i // (per_line - 1)
        j = 1 + lax.rem(i, per_line - 1)
        src = index(lax.rem(along + k, lines), lax.rem(across + j, per_line), 1 - core)
        arrived(src)
        normalize(src)

    mine = pl.ds(pl.multiple_of(me * rows, rows), rows)
    g_part[...] = lax.dot_general(
        nall[mine, :], nall[...], (((1,), (1,)), ((), ())), preferred_element_type=F32
    )

    def gp_copy(k):
        return remote(g_part, g_part_in.at[my_mp], gp_ss.at[k], gp_rs.at[my_mp],
                      {"mp": mp_peer(k)})

    def g_copy(k):
        return remote(g_all.at[mine], g_all.at[mine], g_ss.at[k], g_rs.at[me],
                      {"dp": dp_peer(k)})

    for k in range(1, m):
        gp_copy(k).start()

    @pl.loop(0, chunks)
    def _(i):
        project(1, i)

    cot_copy.wait()
    for k in range(1, m):
        p = mp_peer(k)
        dst = cot_ref.at[pl.ds(pl.multiple_of(p * cot_rows, cot_rows), cot_rows)]
        remote(cot_hbm, dst, cot_ss.at[0], cot_rs.at[p], {"mp": p}).wait_recv()

    def local_groups(part):
        at, size = parts[part]
        for g in range(at // group, (at + size) // group):
            p, a = g // lines, g % lines
            row = (a * per_line + lax.rem(across + p, per_line)) * group
            yield pl.ds(pl.multiple_of(row, group), group)

    def first_slopes(part, i):
        at, size = parts[part]
        off = pl.multiple_of(i * chunk, chunk)
        pre = own[i, pl.ds(at, size)]
        for k in range(1, m):
            p = mp_peer(k)
            remote(sendb.at[i, pl.ds(at, size)], recvb.at[p, i, pl.ds(at, size)],
                   pre_ss.at[part, i, 0], pre_rs.at[part, p, i], {"mp": p}).wait_recv()
            pre = pre + recvb[p, i, pl.ds(at, size)].astype(F32)
        cot = jnp.concatenate([cot_ref[r, pl.ds(off, chunk)] for r in local_groups(part)], axis=0)
        s = (cot.astype(F32) * gelu_slope(pre) * scale).astype(BF16)
        for g, r in enumerate(local_groups(part)):
            pre_ref[r, pl.ds(off, chunk)] = pre[g * group:(g + 1) * group]
            slope[r, pl.ds(off, chunk)] = s[g * group:(g + 1) * group]

    @pl.loop(0, chunks)
    def _(i):
        first_slopes(0, i)

    gram = g_part[...]
    for k in range(1, m):
        p = mp_peer(k)
        remote(g_part, g_part_in.at[p], gp_ss.at[0], gp_rs.at[p], {"mp": p}).wait_recv()
        gram = gram + g_part_in[p]
    g_all[mine, :] = gram

    @pl.loop(1, n)
    def _(k):
        g_copy(k).start()

    @pl.loop(1, n)
    def _(k):
        p = dp_peer(k)
        dst = g_all.at[pl.ds(pl.multiple_of(p * rows, rows), rows)]
        remote(dst, dst, g_ss.at[0], g_rs.at[p], {"dp": p}).wait_recv()

    rest = g_all[...]
    for t in range(3):
        term = rest.astype(BF16)
        g_terms[t * token_count:(t + 1) * token_count] = term
        rest = rest - term.astype(F32)

    nb[me] = jnp.zeros_like(nb[me])

    @pl.loop(0, chunks)
    def _(i):
        first_slopes(1, i)
        off = pl.multiple_of(i * chunk, chunk)
        s = slope[:, pl.ds(off, chunk)]
        t = token_count
        gs = (
            jnp.dot(g_terms[2 * t:], s, preferred_element_type=F32)
            + jnp.dot(g_terms[t:2 * t], s, preferred_element_type=F32)
            + jnp.dot(g_terms[:t], s, preferred_element_type=F32)
        )
        gs_ref[:, pl.ds(off, chunk)] = gs
        nb[me] += jnp.full((8, 128), jnp.sum(gs * s.astype(F32)), F32)

    def nb_copy(k):
        return remote(nb.at[me], nb.at[me], nb_ss.at[k], nb_rs.at[me], {"dp": dp_peer(k)})

    @pl.loop(1, n)
    def _(k):
        nb_copy(k).start()

    @pl.loop(0, depth // 256)
    def _(i):
        off = pl.multiple_of(i * 256, 256)
        nt_ref[pl.ds(off, 256), :] = nall[:, pl.ds(off, 256)].T

    nt_copy = pltpu.make_async_copy(nt_ref, nt_hbm, o_sem.at[0])
    nt_copy.start()

    @pl.loop(1, n)
    def _(k):
        st_copy(k).wait_send()
        g_copy(k).wait_send()

    for pos, low in [(along, True), (along, False)] + by_distance:
        @pl.when(jnp.logical_and(there(pos, low), can_go(low)))
        def _():
            line_copy(pos, low).wait_send()

    @pl.loop(0, lines)
    def _(pos):
        for j in range(per_line):
            core_copy(pos, j).wait_send()
            if j > 0:
                across_copy(pos, j).wait_send()

    for k in range(1, m):
        stp_copy(k).wait_send()
        cot_send(k).wait_send()
        gp_copy(k).wait_send()

        @pl.loop(0, chunks)
        def _(i):
            pre_copy(0, i, k).wait_send()
            pre_copy(1, i, k).wait_send()

    @pl.loop(1, n)
    def _(k):
        p = dp_peer(k)
        remote(nb.at[p], nb.at[p], nb_ss.at[0], nb_rs.at[p], {"dp": p}).wait_recv()
        nb_copy(k).wait_send()

    squared = jnp.sum(nb[...], axis=0)[0:1, 0:1]
    size = jnp.sqrt(jnp.maximum(squared, 0.0)) + 1e-12
    radius = 0.5 * math.sqrt(FF)

    def slope_copy(i):
        at = pl.ds(pl.multiple_of(i * chunk, chunk), chunk)
        return pltpu.make_async_copy(slope.at[:, at], slope_hbm.at[:, at], slope_os.at[i])

    @pl.loop(0, chunks)
    def _(i):
        at = pl.ds(pl.multiple_of(i * chunk, chunk), chunk)
        pre = pre_ref[:, at] + radius * gs_ref[:, at] / size
        slope[:, at] = (cot_ref[:, at].astype(F32) * gelu_slope(pre) * scale).astype(BF16)
        slope_copy(i).start()

    nt_copy.wait()

    @pl.loop(0, chunks)
    def _(i):
        slope_copy(i).wait()


def grad_kernel(nt_hbm, slope_hbm, out_hbm, nt, slope, out, nt_sem, slope_sem, out_sem):
    blocks = nt_sem.shape[0]
    rows = nt.shape[0] // blocks

    def cut(i):
        return pl.ds(pl.multiple_of(i * rows, rows), rows)

    def nt_copy(i):
        return pltpu.make_async_copy(nt_hbm.at[cut(i)], nt.at[cut(i)], nt_sem.at[i])

    def out_copy(i):
        return pltpu.make_async_copy(out.at[cut(i)], out_hbm.at[cut(i)], out_sem.at[i])

    slope_copy = pltpu.make_async_copy(slope_hbm, slope, slope_sem)
    slope_copy.start()

    @pl.loop(0, blocks)
    def _(i):
        nt_copy(i).start()

    slope_copy.wait()

    @pl.loop(0, blocks)
    def _(i):
        nt_copy(i).wait()
        out[cut(i), :] = jnp.dot(nt[cut(i), :], slope[...], preferred_element_type=F32)
        out_copy(i).start()

    @pl.loop(0, blocks)
    def _(i):
        out_copy(i).wait()


def per_device(tokens, norm_gain, w_up, cotangent):
    n, m = lax.axis_size("dp"), lax.axis_size("mp")
    rows, depth = tokens.shape
    count = rows * n
    cols = w_up.shape[1]
    lines = 4
    chunk = next(c for c in (512, 256, 128) if cols % c == 0)
    chunks = cols // chunk
    per_line = n // (2 * lines)
    cot_rows = cotangent.shape[0]
    dma, vmem = pltpu.SemaphoreType.DMA, pltpu.VMEM
    whole = pl.BlockSpec(memory_space=pltpu.VMEM)
    hbm = pl.BlockSpec(memory_space=pl.ANY)
    cfg = (n, m, lines, depth * m, count)
    nt, slope = pl.pallas_call(
        functools.partial(slopes_kernel, cfg),
        out_shape=(
            jax.ShapeDtypeStruct((depth, count), BF16),
            jax.ShapeDtypeStruct((count, cols), BF16),
        ),
        in_specs=[whole, whole, hbm, hbm],
        out_specs=[hbm] * 2,
        scratch_shapes=[
            vmem((depth, count), BF16),
            vmem((count, cols), F32),
            vmem((count, cols), F32),
            vmem((count, cols), BF16),
            vmem((3 * count, count), BF16),
            vmem((count, depth), BF16),
            vmem((n, rows, depth), BF16),
            vmem((count, depth), BF16),
            vmem((depth, cols), BF16),
            vmem((rows, 128), F32),
            vmem((m, rows, 128), F32),
            vmem((n, rows, 128), F32),
            vmem((chunks, count, chunk), F32),
            vmem((chunks, count, chunk), BF16),
            vmem((m, chunks, count, chunk), BF16),
            vmem((rows, count), F32),
            vmem((m, rows, count), F32),
            vmem((count, count), F32),
            vmem((count, cols), BF16),
            vmem((n, 8, 128), F32),
            dma(()), dma(()), dma((1,)), dma((chunks,)),
            dma((2, lines)), dma((lines, per_line)), dma((lines, per_line)),
            dma((n,)),
            dma((m,)), dma((m,)), dma((n,)), dma((n,)), dma((m,)), dma((m,)),
            dma((2, chunks, m)), dma((2, m, chunks)),
            dma((m,)), dma((m,)), dma((n,)), dma((n,)), dma((n,)), dma((n,)),
        ],
        compiler_params=pltpu.CompilerParams(
            collective_id=0, has_side_effects=True, vmem_limit_bytes=56 * 2**20
        ),
        name="slopes",
    )(tokens, norm_gain.reshape(1, depth), w_up, cotangent)

    return pl.pallas_call(
        grad_kernel,
        out_shape=jax.ShapeDtypeStruct((depth, cols), F32),
        in_specs=[hbm, hbm],
        out_specs=hbm,
        scratch_shapes=[
            vmem((depth, count), BF16),
            vmem((count, cols), BF16),
            vmem((depth, cols), F32),
            dma((depth // 256,)), dma(()), dma((depth // 256,)),
        ],
        compiler_params=pltpu.CompilerParams(vmem_limit_bytes=60 * 2**20),
        name="grad",
    )(nt, slope)


def solution(mesh):
    placed = (P("dp", "mp"), P("mp"), P("mp", "dp"), P("mp", "dp"))
    return jax.shard_map(
        per_device, mesh=mesh, in_specs=placed, out_specs=P("mp", "dp"), check_vma=False
    )
```
